256 devices in a mesh: node: 16 (over y, x_hi, core), local: 16 (over x_lo, z).
Axes of the slice: x: 4 (x_hi: 2, x_lo: 2; x = x_hi * 2 + x_lo), y: 4, z: 8, core: 2. Of those that a mesh axis runs over, the one named last changes fastest.
Arguments:
- partials: float32 [256, 638976], P(('node', 'local')), may hold values from -6 to 6
- master: float32 [638976], P(('node', 'local')), may hold values from -4 to 4
- first: float32 [638976], P(('node', 'local')), may hold values from -6 to 6
- second: float32 [638976], P(('node', 'local')), may hold values from 0.02 to 64
- acts: bfloat16 [32768, 6144], P(('node', 'local')), may hold values from -6 to 6
- up_cot: bfloat16 [32768, 6144], P(('node', 'local')), may hold values from -4 to 4
- out_cot: bfloat16 [32768, 6144], P(('node', 'local')), may hold values from -4 to 4
- ln_gain: bfloat16 [6144], replicated, may hold values from 0.5 to 1.5
Outputs:
- new_master: float32 [638976], P(('node', 'local'))
- new_first: float32 [638976], P(('node', 'local'))
- new_second: float32 [638976], P(('node', 'local'))
- new_params: bfloat16 [638976], P('node')
- trust: float32 [64], replicated
- input_grad: bfloat16 [32768, 6144], P(('node', 'local'))
The draws below stay inside these ranges and needn't reach their ends.
All inputs are finite; a program needn't handle non-finite values.
Results may differ from the reference program's by a relative error of at most 0.0004.
Values may be sent and summed in bfloat16 or wider, within the bound.
No kernel may reach another device: no remote copies, remote signals or barrier semaphores. Data moves between devices by JAX's collectives and lax.ppermute only.
A program may use at most 64 MiB of HBM per device.

```python
import math
import jax
import jax.numpy as jnp
from jax import lax

D = 6144
FF = 24576
LAYERS = 8
TOK_DEV = 128
PARAMS = 638976
TOKENS = 32768
N_NODE = 16
N_LOCAL = 16


def draw_first(key, part):
    key = jax.random.fold_in(key, 11)
    key_levels, key_values = jax.random.split(key)
    blocks = PARAMS // 256 + 1
    levels = jnp.exp(jax.random.uniform(key_levels, (blocks,), jnp.float32, -3.0, 1.0))
    block_index = jnp.arange(PARAMS, dtype=jnp.int32) // 256
    values = jax.random.normal(key_values, (PARAMS,), jnp.float32)
    return jnp.clip(values * levels[block_index], -6.0, 6.0)


def draw_second(key, part):
    key = jax.random.fold_in(key, 12)
    key_levels, key_values = jax.random.split(key)
    blocks = PARAMS // 256 + 1
    levels = jax.random.uniform(key_levels, (blocks,), jnp.float32, math.log(0.02), math.log(16.0))
    block_index = jnp.arange(PARAMS, dtype=jnp.int32) // 256
    jitter = jax.random.uniform(key_values, (PARAMS,), jnp.float32, 0.0, math.log(4.0))
    return jnp.clip(jnp.exp(levels[block_index] + jitter), 0.02, 64.0)


def with_spikes(result, own_key, source, target, shards_of, factor):
    owner, partner = [(jnp.arange(result.shape[axis_at]) // (result.shape[axis_at] // shards_of)).reshape([-1 if axis == axis_at else 1 for axis in range(result.ndim)]) for axis_at in (source, target)]
    chosen = jax.random.permutation(own_key, shards_of)[partner]
    strong = (owner == chosen) | (owner == (partner + shards_of // 2) % shards_of)
    return jnp.where(strong, factor * result, result)


def shard_levels(stream_key, extent, pieces, least, top_value):
    gain = 1.0
    for dim, shards_of in pieces:
        steps = jax.random.uniform(jax.random.fold_in(jax.random.fold_in(stream_key, 6), dim), (shards_of,), jnp.float32, least / len(pieces), top_value / len(pieces))
        gain = gain * jnp.repeat(jnp.exp(steps), extent[dim] // shards_of).reshape((-1,) + (1,) * (len(extent) - 1 - dim))
    return gain


def noise(rng, dims, scale, reach, cuts=(), kind=jnp.bfloat16):
    values = scale * jax.random.normal(rng, dims, jnp.float32)
    if cuts:
        values = values * shard_levels(rng, dims, cuts, -0.22, 0.18)
    return jnp.clip(values, -reach, reach).astype(kind)


def bell_draw_with(rng, shape, scale, reach, cuts, heavy, kind=jnp.bfloat16):
    result = scale * jax.random.normal(rng, shape, jnp.float32)
    if cuts:
        result = result * shard_levels(rng, shape, cuts, -0.22, 0.18)
    return jnp.clip(with_spikes(result, jax.random.fold_in(rng, 3), *heavy), -reach, reach).astype(kind)


def setup_inputs(seed: int = 0) -> dict:
    streams_of = jax.random.split(jax.random.key(seed), 9)
    return {
        "partials": bell_draw_with(streams_of[0], (N_NODE * N_LOCAL, PARAMS), 0.25, 6.0, ((0, 256),), (0, 1, 256, 6.0), jnp.float32),
        "master": noise(streams_of[1], (PARAMS,), 0.5, 4.0, ((0, 256),), jnp.float32),
        "first": draw_first(jax.random.fold_in(streams_of[8], 71), 0),
        "second": draw_second(jax.random.fold_in(streams_of[8], 71), 0),
        "acts": noise(streams_of[4], (TOKENS, D), 1.0, 6.0, ((0, 256),)),
        "up_cot": noise(streams_of[5], (TOKENS, D), 0.5, 4.0, ((0, 256),)),
        "out_cot": noise(streams_of[6], (TOKENS, D), 0.5, 4.0, ((0, 256),)),
        "ln_gain": jnp.clip(1.0 + 0.1 * jax.random.normal(streams_of[7], (D,), jnp.float32), 0.5, 1.5).astype(jnp.bfloat16),
    }


beta_one = 0.9
beta_two = 0.999
adam_epsilon = 1e-06
norm_epsilon = 1e-05
learn_rate = 0.01

def tensor_ids(position, width, hidden, length):
    layer = position // length
    offset = position - layer * length
    bounds = (width, 2 * width, 5 * width, 6 * width, 7 * width, 8 * width, 8 * width + hidden)
    kind = jnp.zeros_like(position)
    for bound in bounds:
        kind = kind + (offset >= bound).astype(jnp.int32)
    return layer * 8 + kind

def last_layer(acts, up_cot, out_cot, ln_gain):
    values = acts.astype(jnp.float32)
    center = lax.optimization_barrier(jnp.mean(values, axis=-1, keepdims=True))
    centered = values - center
    variance = lax.optimization_barrier(jnp.mean(centered * centered, axis=-1, keepdims=True))
    inverse = lax.rsqrt(variance + norm_epsilon)
    normed = centered * inverse
    upward = up_cot.astype(jnp.float32)
    outward = out_cot.astype(jnp.float32)
    gain_part = lax.optimization_barrier(jnp.sum(upward * normed, axis=0))
    shift_part = lax.optimization_barrier(jnp.sum(upward, axis=0))
    bias_part = lax.optimization_barrier(jnp.sum(outward, axis=0))
    scaled = upward * ln_gain.astype(jnp.float32)
    inner = scaled - lax.optimization_barrier(jnp.mean(scaled, axis=-1, keepdims=True)) - normed * lax.optimization_barrier(jnp.mean(scaled * normed, axis=-1, keepdims=True))
    input_grad = (outward + inverse * inner).astype(jnp.bfloat16)
    return (gain_part, shift_part, bias_part, input_grad)

def place_last(flat, gain_part, shift_part, bias_part, width, hidden, length, layers):
    base = (layers - 1) * length
    flat = flat.at[base + 6 * width:base + 7 * width].add(gain_part)
    flat = flat.at[base + 7 * width:base + 8 * width].add(shift_part)
    flat = flat.at[base + 8 * width + hidden:base + 9 * width + hidden].add(bias_part)
    return flat

def reference(partials, master, first, second, acts, up_cot, out_cot, ln_gain):
    devices = N_NODE * N_LOCAL
    length = 9 * D + FF

    def one_block(item):
        return last_layer(item[0], item[1], item[2], ln_gain)
    blocks = lax.map(one_block, (acts.reshape(devices, TOK_DEV, D), up_cot.reshape(devices, TOK_DEV, D), out_cot.reshape(devices, TOK_DEV, D)))
    gain_part = lax.optimization_barrier(jnp.sum(blocks[0], axis=0))
    shift_part = lax.optimization_barrier(jnp.sum(blocks[1], axis=0))
    bias_part = lax.optimization_barrier(jnp.sum(blocks[2], axis=0))
    input_grad = blocks[3].reshape(TOKENS, D)
    grad = lax.optimization_barrier(jnp.sum(partials, axis=0))
    grad = place_last(grad, gain_part, shift_part, bias_part, D, FF, length, LAYERS)
    new_first = beta_one * first + (1.0 - beta_one) * grad
    new_second = beta_two * second + (1.0 - beta_two) * grad * grad
    update = new_first / (jnp.sqrt(new_second) + adam_epsilon)
    ids = tensor_ids(jnp.arange(PARAMS, dtype=jnp.int32), D, FF, length)
    count = 8 * LAYERS
    weight_sq = jax.ops.segment_sum(master * master, ids, count)
    update_sq = jax.ops.segment_sum(update * update, ids, count)
    trust = jnp.sqrt(weight_sq) / (jnp.sqrt(update_sq) + adam_epsilon)
    new_master = master - learn_rate * trust[ids] * update
    return (new_master, new_first, new_second, new_master.astype(jnp.bfloat16), trust, input_grad)
```

```python
import jax
import jax.numpy as jnp
from jax import lax
from jax.experimental import pallas as pl
from jax.experimental.pallas import tpu as pltpu
from jax.sharding import Mesh, PartitionSpec as P

D = 6144
FF = 24576
LAYERS = 8
LENGTH = 9 * D + FF
PARAMS = LAYERS * LENGTH
LANES = 128
NODES = 16
LOCALS = 16
SHARD = PARAMS // (NODES * LOCALS)
NODE_PART = PARAMS // NODES
NODE_ROWS = NODE_PART // LANES
CHUNK_ROWS = NODE_ROWS // 2
CHUNK_PAD = 160
PIECE = 24
PAIR_ROWS = 2 * SHARD // LANES
BOUNDS = (0, D, 2 * D, 5 * D, 6 * D, 7 * D, 8 * D, 8 * D + FF, LENGTH)

beta_one = 0.9
beta_two = 0.999
adam_epsilon = 1e-06
norm_epsilon = 1e-05
learn_rate = 0.01

f32 = jnp.float32
TOKENS_STEP = 32
COLS = D // LANES
VMEM_LIMIT = 48 * 1024 * 1024


def whole():
    return pl.BlockSpec(memory_space=pltpu.VMEM)


def params():
    return pltpu.CompilerParams(vmem_limit_bytes=VMEM_LIMIT)


def norm_kernel(acts, up, out, gain, grad, parts, sums):
    step = pl.program_id(0)
    rows = acts.shape[0]

    def cols(j):
        return slice(j * LANES, (j + 1) * LANES)

    total = jnp.zeros((rows, LANES), f32)
    for j in range(COLS):
        total = total + acts[:, cols(j)].astype(f32)
    center = jnp.broadcast_to(jnp.sum(total, axis=1, keepdims=True) * (1.0 / D), (rows, LANES))
    squares = jnp.zeros((rows, LANES), f32)
    scaled = jnp.zeros((rows, LANES), f32)
    cross = jnp.zeros((rows, LANES), f32)
    for j in range(COLS):
        x = acts[:, cols(j)].astype(f32) - center
        s = up[:, cols(j)].astype(f32) * gain[:, cols(j)].astype(f32)
        squares = squares + x * x
        scaled = scaled + s
        cross = cross + s * x
    variance = jnp.sum(squares, axis=1, keepdims=True) * (1.0 / D)
    inverse_col = lax.rsqrt(variance + norm_epsilon)
    mean_scaled = jnp.sum(scaled, axis=1, keepdims=True) * (1.0 / D)
    mean_cross = jnp.sum(cross, axis=1, keepdims=True) * (1.0 / D) * inverse_col
    inverse = jnp.broadcast_to(inverse_col, (rows, LANES))
    mean_scaled = jnp.broadcast_to(mean_scaled, (rows, LANES))
    mean_cross = jnp.broadcast_to(mean_cross, (rows, LANES))

    def fold(v):
        return jnp.sum(v.reshape(rows // 8, 8, LANES), axis=0)

    @pl.when(step == 0)
    def _():
        sums[...] = jnp.zeros_like(sums)

    for j in range(COLS):
        normed = (acts[:, cols(j)].astype(f32) - center) * inverse
        u = up[:, cols(j)].astype(f32)
        o = out[:, cols(j)].astype(f32)
        inner = u * gain[:, cols(j)].astype(f32) - mean_scaled - normed * mean_cross
        grad[:, cols(j)] = (o + inverse * inner).astype(jnp.bfloat16)
        sums[0, :, cols(j)] += fold(u * normed)
        sums[1, :, cols(j)] += fold(u)
        sums[2, :, cols(j)] += fold(o)

    @pl.when(step == pl.num_programs(0) - 1)
    def _():
        for which in range(3):
            for j in range(COLS):
                row = which * COLS + j
                parts[row : row + 1, :] = jnp.sum(sums[which, :, cols(j)], axis=0, keepdims=True)


def norm_backward(acts, up, out, gain):
    tokens = acts.shape[0]
    block = pl.BlockSpec((TOKENS_STEP, D), lambda i: (i, 0))
    return pl.pallas_call(
        norm_kernel,
        grid=(tokens // TOKENS_STEP,),
        in_specs=[block, block, block, pl.BlockSpec((1, D), lambda i: (0, 0))],
        out_specs=[block, pl.BlockSpec((3 * COLS, LANES), lambda i: (0, 0))],
        out_shape=[
            jax.ShapeDtypeStruct((tokens, D), jnp.bfloat16),
            jax.ShapeDtypeStruct((3 * COLS, LANES), f32),
        ],
        scratch_shapes=[pltpu.VMEM((3, 8, D), f32)],
        compiler_params=params(),
        cost_estimate=pl.CostEstimate(flops=30 * tokens * D, bytes_accessed=8 * tokens * D, transcendentals=0),
    )(acts, up, out, gain.reshape(1, D))


def pair_kernel(core, own, other, parts, parts_other, result):
    step = pl.program_id(0)
    result[0, 0, 0:CHUNK_ROWS, :] = own[0, 0, 0:CHUNK_ROWS, :] + other[0, 0:CHUNK_ROWS, :]
    result[0, 1, 0:CHUNK_ROWS, :] = own[0, 0, CHUNK_ROWS:NODE_ROWS, :] + other[0, CHUNK_ROWS:NODE_ROWS, :]
    for half in range(2):
        result[0, half, CHUNK_ROWS:CHUNK_PAD, :] = jnp.zeros((CHUNK_PAD - CHUNK_ROWS, LANES), f32)

    def add(half, row, first, count):
        total = parts[first : first + count, :] + parts_other[first : first + count, :]
        result[0, half, row : row + count, :] += total

    @pl.when((step == pl.num_programs(0) - 1) & (core[0] == 0))
    def _():
        add(1, CHUNK_ROWS - COLS // 2, 0, COLS // 2)

    @pl.when((step == pl.num_programs(0) - 1) & (core[0] == 1))
    def _():
        add(0, 0, COLS // 2, COLS // 2)
        add(0, COLS // 2, COLS, COLS)
        add(1, CHUNK_ROWS - COLS, 2 * COLS, COLS)


def pair_sum(core, grid, other, parts, parts_other):
    small = pl.BlockSpec((3 * COLS, LANES), lambda i, c: (0, 0))
    return pl.pallas_call(
        pair_kernel,
        grid_spec=pltpu.PrefetchScalarGridSpec(
            num_scalar_prefetch=1,
            grid=(NODES // 2,),
            in_specs=[
                pl.BlockSpec((1, 1, NODE_ROWS, LANES), lambda i, c: (i, c[0], 0, 0)),
                pl.BlockSpec((1, NODE_ROWS, LANES), lambda i, c: (i, 0, 0)),
                small,
                small,
            ],
            out_specs=pl.BlockSpec((1, 2, CHUNK_PAD, LANES), lambda i, c: (i, 0, 0, 0)),
        ),
        out_shape=jax.ShapeDtypeStruct((NODES // 2, 2, CHUNK_PAD, LANES), f32),
        compiler_params=params(),
    )(core, grid, other, parts, parts_other)


def lane_index(rows):
    return lax.broadcasted_iota(jnp.int32, (rows, LANES), 1)


def split_kernel(blocks, pieces, total):
    total[...] = jnp.sum(blocks[...], axis=0)
    high = lane_index(20) >= LANES // 2
    for z in range(8):
        base = PAIR_ROWS * (z // 2)
        if z % 2 == 0:
            piece = total[base : base + 20, :]
        else:
            start = base + PAIR_ROWS // 2
            piece = pltpu.roll(
                jnp.where(high, total[start : start + 20, :], total[start + 1 : start + 21, :]), LANES // 2, 1
            )
        pieces[z, 0:20, :] = piece
        pieces[z, 20:PIECE, :] = jnp.zeros((PIECE - 20, LANES), f32)


def split_sum(blocks):
    return pl.pallas_call(
        split_kernel,
        in_specs=[whole()],
        out_specs=whole(),
        out_shape=jax.ShapeDtypeStruct((8, PIECE, LANES), f32),
        scratch_shapes=[pltpu.VMEM((CHUNK_PAD, LANES), f32)],
        compiler_params=params(),
    )(blocks)


def step_kernel(pieces, master, first, second, new_first, new_second, message):
    grad = jnp.sum(pieces[...], axis=0)
    moment = beta_one * first[...] + (1.0 - beta_one) * grad
    spread = beta_two * second[...] + (1.0 - beta_two) * grad * grad
    new_first[...] = moment
    new_second[...] = spread
    update = moment / (jnp.sqrt(spread) + adam_epsilon)
    held = master[...]
    for i in range(LOCALS):
        message[i, 0:PIECE, :] = update
        message[i, PIECE : 2 * PIECE, :] = held


def step(pieces, master, first, second):
    shard = jax.ShapeDtypeStruct((PIECE, LANES), f32)
    return pl.pallas_call(
        step_kernel,
        in_specs=[whole()] * 4,
        out_specs=[whole()] * 3,
        out_shape=[shard, shard, jax.ShapeDtypeStruct((LOCALS, 2 * PIECE, LANES), f32)],
        compiler_params=params(),
    )(pieces, master, first, second)


def kinds_of(piece):
    found = set()
    for half in range(2):
        low = half * NODE_PART + piece * SHARD
        high = low + SHARD
        found |= {k for k in range(8) if BOUNDS[k] < high and BOUNDS[k + 1] > low}
    return sorted(found)


def place(rows):
    return lax.broadcasted_iota(jnp.int32, (rows, LANES), 0) * LANES + lane_index(rows)


def sums_kernel(core, gathered, message):
    start = core[0] * NODE_PART
    inside = place(PIECE)
    valid = inside < SHARD
    weights = [jnp.zeros((8, LANES), f32) for _ in range(8)]
    updates = [jnp.zeros((8, LANES), f32) for _ in range(8)]
    for i in range(LOCALS):
        offset = inside + (start + i * SHARD)
        update = gathered[i, 0:PIECE, :]
        held = gathered[i, PIECE : 2 * PIECE, :]
        update_sq = jnp.where(valid, update * update, 0.0)
        held_sq = jnp.where(valid, held * held, 0.0)
        for k in kinds_of(i):
            mask = (offset >= BOUNDS[k]) & (offset < BOUNDS[k + 1])
            weights[k] += jnp.sum(jnp.where(mask, held_sq, 0.0).reshape(3, 8, LANES), axis=0)
            updates[k] += jnp.sum(jnp.where(mask, update_sq, 0.0).reshape(3, 8, LANES), axis=0)
    rows = [jnp.sum(v, axis=0, keepdims=True) for v in weights + updates]
    table = jnp.concatenate(rows, axis=0)
    for i in range(NODES):
        message[i, :, :] = table


def node_sums(core, gathered):
    return pl.pallas_call(
        sums_kernel,
        in_specs=[pl.BlockSpec(memory_space=pltpu.SMEM), whole()],
        out_specs=whole(),
        out_shape=jax.ShapeDtypeStruct((NODES, 16, LANES), f32),
        compiler_params=params(),
    )(core, gathered)


def final_kernel(where, tables, gathered, new_master, new_params, trust, masters, flat, shifted):
    core, layer, mine = where[0], where[1], where[2]
    for n in range(LAYERS):
        table = tables[2 * n, :, :] + tables[2 * n + 1, :, :]
        weight_sq = jnp.sum(table[0:8, :], axis=1, keepdims=True)
        update_sq = jnp.sum(table[8:16, :], axis=1, keepdims=True)
        ratio = jnp.sqrt(weight_sq) / (jnp.sqrt(update_sq) + adam_epsilon)
        trust[n, :, :] = jnp.broadcast_to(ratio, (8, LANES))
    ratios = trust[layer]
    start = core * NODE_PART
    inside = place(PIECE)
    for i in range(LOCALS):
        offset = inside + (start + i * SHARD)
        kinds = kinds_of(i)
        factor = jnp.broadcast_to(ratios[kinds[0] : kinds[0] + 1, :], (PIECE, LANES))
        for k in kinds[1:]:
            factor = jnp.where(offset >= BOUNDS[k], ratios[k : k + 1, :], factor)
        masters[i, :, :] = gathered[i, PIECE : 2 * PIECE, :] - learn_rate * factor * gathered[i, 0:PIECE, :]
    new_master[...] = masters[mine]
    low = lane_index(20) < LANES // 2
    for k in range(LOCALS // 2):
        base = PAIR_ROWS * k
        flat[base : base + 19, :] = masters[2 * k, 0:19, :]
        shifted[0:1, :] = masters[2 * k, 19:20, :]
        shifted[1:21, :] = pltpu.roll(masters[2 * k + 1, 0:20, :], LANES // 2, 1)
        flat[base + 19 : base + 39, :] = jnp.where(low, shifted[0:20, :], shifted[1:21, :])
    new_params[...] = flat[...].astype(jnp.bfloat16)


def finish(where, tables, gathered):
    return pl.pallas_call(
        final_kernel,
        in_specs=[pl.BlockSpec(memory_space=pltpu.SMEM), whole(), whole()],
        out_specs=[whole()] * 3,
        out_shape=[
            jax.ShapeDtypeStruct((PIECE, LANES), f32),
            jax.ShapeDtypeStruct((NODE_ROWS, LANES), jnp.bfloat16),
            jax.ShapeDtypeStruct((LAYERS, 8, LANES), f32),
        ],
        scratch_shapes=[
            pltpu.VMEM((LOCALS, PIECE, LANES), f32),
            pltpu.VMEM((NODE_ROWS, LANES), f32),
            pltpu.VMEM((24, LANES), f32),
        ],
        compiler_params=params(),
    )(where, tables, gathered)


def padded(vector):
    return jnp.pad(vector, (0, PIECE * LANES - SHARD)).reshape(PIECE, LANES)


def local(partials, master, first, second, acts, up_cot, out_cot, ln_gain):
    core = lax.axis_index("c")
    node = (lax.axis_index("y") * 2 + lax.axis_index("xh")) * 2 + core
    mine = lax.axis_index("xl") * 8 + lax.axis_index("z")
    swap = ((0, 1), (1, 0))
    core_scalar = core.astype(jnp.int32).reshape(1)
    where = jnp.stack([core, node // 2, mine]).astype(jnp.int32)

    grid = partials.reshape(NODES // 2, 2, NODE_ROWS, LANES)
    sent = lax.dynamic_index_in_dim(grid, 1 - core, axis=1, keepdims=False)
    other = lax.ppermute(sent, "c", swap)
    input_grad, parts = norm_backward(acts, up_cot, out_cot, ln_gain)
    parts_other = lax.ppermute(parts, "c", swap)
    chunks = pair_sum(core_scalar, grid, other, parts, parts_other)
    chunks = chunks.reshape(NODES, CHUNK_PAD, LANES)
    blocks = lax.all_to_all(chunks, ("y", "xh", "xl"), 0, 0, tiled=True)
    pieces = lax.all_to_all(split_sum(blocks), "z", 0, 0, tiled=True)
    new_first, new_second, message = step(pieces, padded(master), padded(first), padded(second))
    gathered = lax.all_to_all(message, ("xl", "z"), 0, 0, tiled=True)
    tables = lax.all_to_all(node_sums(core_scalar, gathered), ("y", "xh", "c"), 0, 0, tiled=True)
    new_master, new_params, trust = finish(where, tables, gathered)

    def flat(piece):
        return piece.reshape(PIECE * LANES)[:SHARD]

    return (
        flat(new_master),
        flat(new_first),
        flat(new_second),
        new_params.reshape(NODE_PART),
        trust[:, :, 0].reshape(8 * LAYERS),
        input_grad,
    )


def solution(mesh):
    fine = Mesh(mesh.devices.reshape(4, 2, 2, 2, 8), ("y", "xh", "c", "xl", "z"))
    every = ("y", "xh", "c", "xl", "z")
    in_specs = (P(every, None), P(every), P(every), P(every), P(every, None), P(every, None), P(every, None), P())
    out_specs = (P(every), P(every), P(every), P(("y", "xh", "c")), P(), P(every, None))
    return jax.shard_map(local, mesh=fine, in_specs=in_specs, out_specs=out_specs, check_vma=False)
```

```python
import jax
import jax.numpy as jnp
from jax import lax
from jax.experimental import pallas as pl
from jax.experimental.pallas import tpu as pltpu
from jax.sharding import Mesh, PartitionSpec as P

D = 6144
FF = 24576
LAYERS = 8
LENGTH = 9 * D + FF
PARAMS = LAYERS * LENGTH
LANES = 128
NODES = 16
LOCALS = 16
SHARD = PARAMS // (NODES * LOCALS)
NODE_PART = PARAMS // NODES
NODE_ROWS = NODE_PART // LANES
CHUNK_ROWS = NODE_ROWS // 2
CHUNK_PAD = 160
PIECE = 24
QUARTER = LENGTH // 4
SHARD_ROWS = 20
PAIR_ROWS = 2 * SHARD // LANES
BOUNDS = (0, D, 2 * D, 5 * D, 6 * D, 7 * D, 8 * D, 8 * D + FF, LENGTH)

beta_one = 0.9
beta_two = 0.999
adam_epsilon = 1e-06
norm_epsilon = 1e-05
learn_rate = 0.01

f32 = jnp.float32
f16 = jnp.float16
SCALE = 256.0
PARTS_SCALE = 1.0 / 32.0
LOW_SCALE = 2048.0
TOKENS_STEP = 32
COLS = D // LANES
VMEM_LIMIT = 16 * 1024 * 1024
SUMS_VMEM_LIMIT = 55 * 1024 * 1024


def whole():
    return pl.BlockSpec(memory_space=pltpu.VMEM)


def params(limit=VMEM_LIMIT):
    return pltpu.CompilerParams(vmem_limit_bytes=limit)


def cols(j):
    return slice(j * LANES, (j + 1) * LANES)


def wide(column):
    return jnp.broadcast_to(column, (column.shape[0], LANES))


def parts_kernel(acts, up, out, parts, center_rows, inverse_rows, acts_buf, up_buf, out_buf, sums, sems):
    steps = acts.shape[0] // TOKENS_STEP

    def copies(i):
        rows = pl.ds(pl.multiple_of(i * TOKENS_STEP, TOKENS_STEP), TOKENS_STEP)
        pairs = ((acts, acts_buf), (up, up_buf), (out, out_buf))
        return [pltpu.make_async_copy(a.at[rows], b.at[rows], sems.at[k, i]) for k, (a, b) in enumerate(pairs)]

    for i in range(steps):
        for copy in copies(i):
            copy.start()
    sums[...] = jnp.zeros_like(sums)

    def fold(v):
        return jnp.sum(v.reshape(TOKENS_STEP // 8, 8, LANES), axis=0)

    def body(i, carry):
        rows = pl.ds(pl.multiple_of(i * TOKENS_STEP, TOKENS_STEP), TOKENS_STEP)
        for copy in copies(i):
            copy.wait()
        total = jnp.zeros((TOKENS_STEP, LANES), f32)
        for j in range(COLS):
            total = total + acts_buf[rows, cols(j)].astype(f32)
        center = wide(jnp.sum(total, axis=1, keepdims=True) * (1.0 / D))
        squares = jnp.zeros((TOKENS_STEP, LANES), f32)
        for j in range(COLS):
            x = acts_buf[rows, cols(j)].astype(f32) - center
            squares = squares + x * x
        variance = jnp.sum(squares, axis=1, keepdims=True) * (1.0 / D)
        inverse = wide(lax.rsqrt(variance + norm_epsilon))
        center_rows[rows, :] = center
        inverse_rows[rows, :] = inverse
        for j in range(COLS):
            normed = (acts_buf[rows, cols(j)].astype(f32) - center) * inverse
            u = up_buf[rows, cols(j)].astype(f32)
            sums[0, :, cols(j)] += fold(u * normed)
            sums[1, :, cols(j)] += fold(u)
            sums[2, :, cols(j)] += fold(out_buf[rows, cols(j)].astype(f32))
        return carry

    lax.fori_loop(0, steps, body, 0)
    for which in range(3):
        for j in range(COLS):
            row = which * COLS + j
            parts[row : row + 1, :] = jnp.sum(sums[which, :, cols(j)], axis=0, keepdims=True)


def token_sums(acts, up, out):
    tokens = acts.shape[0]
    hbm = pl.BlockSpec(memory_space=pltpu.HBM)
    return pl.pallas_call(
        parts_kernel,
        in_specs=[hbm, hbm, hbm],
        out_specs=[whole()] * 3,
        out_shape=[
            jax.ShapeDtypeStruct((3 * COLS, LANES), f32),
            jax.ShapeDtypeStruct((tokens, LANES), f32),
            jax.ShapeDtypeStruct((tokens, LANES), f32),
        ],
        scratch_shapes=[pltpu.VMEM((tokens, D), jnp.bfloat16)] * 3
        + [pltpu.VMEM((3, 8, D), f32), pltpu.SemaphoreType.DMA((3, tokens // TOKENS_STEP))],
        compiler_params=params(SUMS_VMEM_LIMIT),
        cost_estimate=pl.CostEstimate(flops=15 * tokens * D, bytes_accessed=6 * tokens * D, transcendentals=0),
    )(acts, up, out)


def grad_kernel(acts, up, out, gain, center_rows, inverse_rows, grad):
    rows = acts.shape[0]
    center = center_rows[...]
    inverse = inverse_rows[...]
    scaled = jnp.zeros((rows, LANES), f32)
    cross = jnp.zeros((rows, LANES), f32)
    for j in range(COLS):
        s = up[:, cols(j)].astype(f32) * gain[:, cols(j)].astype(f32)
        scaled = scaled + s
        cross = cross + s * (acts[:, cols(j)].astype(f32) - center)
    mean_scaled = wide(jnp.sum(scaled, axis=1, keepdims=True) * (1.0 / D))
    mean_cross = wide(jnp.sum(cross, axis=1, keepdims=True) * (1.0 / D)) * inverse
    for j in range(COLS):
        normed = (acts[:, cols(j)].astype(f32) - center) * inverse
        s = up[:, cols(j)].astype(f32) * gain[:, cols(j)].astype(f32)
        inner = s - mean_scaled - normed * mean_cross
        grad[:, cols(j)] = (out[:, cols(j)].astype(f32) + inverse * inner).astype(jnp.bfloat16)


def input_gradient(acts, up, out, gain, center_rows, inverse_rows):
    tokens = acts.shape[0]
    block = pl.BlockSpec((TOKENS_STEP, D), lambda i: (i, 0))
    rows = pl.BlockSpec((TOKENS_STEP, LANES), lambda i: (i, 0))
    return pl.pallas_call(
        grad_kernel,
        grid=(tokens // TOKENS_STEP,),
        in_specs=[block, block, block, pl.BlockSpec((1, D), lambda i: (0, 0)), rows, rows],
        out_specs=block,
        out_shape=jax.ShapeDtypeStruct((tokens, D), jnp.bfloat16),
        compiler_params=params(),
        cost_estimate=pl.CostEstimate(flops=15 * tokens * D, bytes_accessed=8 * tokens * D, transcendentals=0),
    )(acts, up, out, gain.reshape(1, D), center_rows, inverse_rows)


def pair_kernel(core, grid, other, parts, parts_other, result, own_buf, other_buf, parts_buf, sems, parts_sems):
    own_copies = [
        pltpu.make_async_copy(grid.at[i, core[0]], own_buf.at[i], sems.at[0, i]) for i in range(NODES // 2)
    ]
    other_copies = [pltpu.make_async_copy(other.at[i], other_buf.at[i], sems.at[1, i]) for i in range(NODES // 2)]
    parts_copies = [
        pltpu.make_async_copy(source, parts_buf.at[k], parts_sems.at[k])
        for k, source in enumerate((parts, parts_other))
    ]
    for own, theirs in zip(own_copies, other_copies):
        own.start()
        theirs.start()
    for copy in parts_copies:
        copy.start()

    def pair(i, half, low, high):
        rows = slice(half * CHUNK_ROWS + low, half * CHUNK_ROWS + high)
        return own_buf[i, rows, :] + other_buf[i, rows, :]

    for i in range(NODES // 2):
        own_copies[i].wait()
        other_copies[i].wait()
        for half in range(2):
            result[i, half, 0:CHUNK_ROWS, :] = pair(i, half, 0, CHUNK_ROWS) * SCALE
            result[i, half, CHUNK_ROWS:CHUNK_PAD, :] = jnp.zeros((CHUNK_PAD - CHUNK_ROWS, LANES), f32)
    for copy in parts_copies:
        copy.wait()
    last = NODES // 2 - 1

    def add(half, row, first, count):
        total = parts_buf[0, first : first + count, :] + parts_buf[1, first : first + count, :]
        result[last, half, row : row + count, :] = (pair(last, half, row, row + count) + total) * PARTS_SCALE

    @pl.when(core[0] == 0)
    def _():
        add(1, CHUNK_ROWS - COLS // 2, 0, COLS // 2)

    @pl.when(core[0] == 1)
    def _():
        add(0, 0, COLS // 2, 3 * COLS // 2)
        add(1, CHUNK_ROWS - COLS, 2 * COLS, COLS)


def pair_sum(core, grid, other, parts, parts_other):
    hbm = pl.BlockSpec(memory_space=pltpu.HBM)
    return pl.pallas_call(
        pair_kernel,
        in_specs=[pl.BlockSpec(memory_space=pltpu.SMEM), hbm, hbm, hbm, hbm],
        out_specs=whole(),
        out_shape=jax.ShapeDtypeStruct((NODES // 2, 2, CHUNK_PAD, LANES), f32),
        scratch_shapes=[
            pltpu.VMEM((NODES // 2, NODE_ROWS, LANES), f32),
            pltpu.VMEM((NODES // 2, NODE_ROWS, LANES), f32),
            pltpu.VMEM((2, 3 * COLS, LANES), f32),
            pltpu.SemaphoreType.DMA((2, NODES // 2)),
            pltpu.SemaphoreType.DMA((2,)),
        ],
        compiler_params=params(),
    )(core, grid, other, parts, parts_other)


def lane_index(rows):
    return lax.broadcasted_iota(jnp.int32, (rows, LANES), 1)


def flatten(states, first, flat, shifted):
    low = lane_index(20) < LANES // 2
    for k in range(4):
        base = PAIR_ROWS * k
        flat[base : base + 19, :] = states[2 * k, first : first + 19, :]
        shifted[0:1, :] = states[2 * k, first + 19 : first + 20, :]
        shifted[1:21, :] = pltpu.roll(states[2 * k + 1, first : first + 20, :], LANES // 2, 1)
        flat[base + 19 : base + 39, :] = jnp.where(low, shifted[0:20, :], shifted[1:21, :])
    flat[CHUNK_ROWS:CHUNK_PAD, :] = jnp.zeros((CHUNK_PAD - CHUNK_ROWS, LANES), f32)


def own_shard(flat, z):
    odd = lax.rem(z, 2)
    start = PAIR_ROWS * lax.div(z, 2) + odd * 19
    ahead = flat[pl.ds(start, 20), :]
    behind = flat[pl.ds(start + 1, 20), :]
    moved = pltpu.roll(jnp.where(lane_index(20) >= LANES // 2, ahead, behind), LANES // 2, 1)
    return jnp.where(odd == 1, moved, ahead)


def bounds_of(quarter):
    edges = BOUNDS + (LENGTH,)
    result = []
    for j in range(4):
        edge = jnp.int32(edges[j])
        for q in range(1, 4):
            edge = jnp.where(quarter == q, edges[2 * q + j] - q * QUARTER, edge)
        result.append(edge)
    return result


def place(rows):
    return lax.broadcasted_iota(jnp.int32, (rows, LANES), 0) * LANES + lane_index(rows)


def moments(first, second, grad):
    new_first = beta_one * first + (1.0 - beta_one) * grad
    new_second = beta_two * second + (1.0 - beta_two) * grad * grad
    return new_first, new_second, new_first / (jnp.sqrt(new_second) + adam_epsilon)


def step_kernel(where, total, states, own_first, own_second, new_first, new_second, sent, table, own_update, flats, shifted):
    layer, quarter, z = where[0], where[1], where[2]
    offset = place(CHUNK_PAD)
    for i in range(4):
        flatten(states, SHARD_ROWS * i, flats.at[i], shifted)
    inside = offset + quarter * QUARTER
    added = ((inside >= BOUNDS[4]) & (inside < BOUNDS[6])) | (inside >= BOUNDS[7])
    added = added & (layer == LAYERS - 1)
    grad = total[...] * jnp.where(added, 1.0 / PARTS_SCALE, 1.0 / SCALE)
    update = moments(flats[0], flats[1], grad)[2]
    held = flats[2] + flats[3] * (1.0 / LOW_SCALE)
    sent[0, :, :] = update
    sent[1, :, :] = held
    edges = bounds_of(quarter)
    rows = []
    for value in (held, update):
        square = value * value
        for j in range(3):
            mask = (offset >= edges[j]) & (offset < edges[j + 1])
            rows.append(jnp.sum(jnp.where(mask, square, 0.0), axis=0, keepdims=True))
    sums = jnp.concatenate(rows + [jnp.zeros((2, LANES), f32)], axis=0)
    for i in range(32):
        table[i, :, :] = sums
    flats[0, :, :] = grad
    first, second, update = moments(
        own_first[0:SHARD_ROWS, :], own_second[0:SHARD_ROWS, :], own_shard(flats.at[0], z)
    )
    new_first[0:SHARD_ROWS, :] = first
    new_second[0:SHARD_ROWS, :] = second
    own_update[0:SHARD_ROWS, :] = update


def step(where, total, states, first, second):
    shard = jax.ShapeDtypeStruct((PIECE, LANES), f32)
    return pl.pallas_call(
        step_kernel,
        in_specs=[pl.BlockSpec(memory_space=pltpu.SMEM)] + [whole()] * 4,
        out_specs=[whole()] * 5,
        out_shape=[
            shard,
            shard,
            jax.ShapeDtypeStruct((2, CHUNK_PAD, LANES), f32),
            jax.ShapeDtypeStruct((32, 8, LANES), f32),
            shard,
        ],
        scratch_shapes=[pltpu.VMEM((4, CHUNK_PAD, LANES), f32), pltpu.VMEM((24, LANES), f32)],
        compiler_params=params(),
    )(where, total, states, first, second)


def final_kernel(where, tables, own, other, own_master, own_update, new_master, new_params, trust, factors, flat, ratios):
    layer, quarter, z = where[0], where[1], where[2]
    xlo = lax.rem(quarter, 2)
    weight_rows, update_rows = [], []
    for n in range(LAYERS):
        quarters = [tables[4 * n + q, :, :] for q in range(4)]
        for k in range(8):
            q, j = k // 2, k % 2
            for rows, first in ((weight_rows, 0), (update_rows, 3)):
                value = quarters[q][first + j : first + j + 1, :]
                if j == 0 and q > 0:
                    value = value + quarters[q - 1][first + 2 : first + 3, :]
                rows.append(value)
    weight_sq = jnp.sum(jnp.concatenate(weight_rows, axis=0), axis=1, keepdims=True)
    update_sq = jnp.sum(jnp.concatenate(update_rows, axis=0), axis=1, keepdims=True)
    ratio = jnp.sqrt(weight_sq) / (jnp.sqrt(update_sq) + adam_epsilon)
    ratios[...] = jnp.broadcast_to(ratio, (8 * LAYERS, LANES))
    diagonal = lane_index(8 * LAYERS) == lax.broadcasted_iota(jnp.int32, (8 * LAYERS, LANES), 0)
    trust[...] = jnp.sum(jnp.where(diagonal, ratios[...], 0.0), axis=0, keepdims=True)
    offset = place(CHUNK_PAD)

    def factor_of(q):
        edges = bounds_of(q)
        rows = [ratios[pl.ds(8 * layer + lax.min(2 * q + j, 7), 1), :] for j in range(3)]
        factor = jnp.broadcast_to(rows[0], (CHUNK_PAD, LANES))
        for j in (1, 2):
            factor = jnp.where(offset >= edges[j], rows[j], factor)
        return factor

    factor = factor_of(quarter)
    mine = own[1, :, :] - learn_rate * factor * own[0, :, :]
    theirs = other[1, :, :] - learn_rate * factor_of(quarter + 1 - 2 * xlo) * other[0, :, :]
    flat[0:CHUNK_ROWS, :] = jnp.where(xlo == 0, mine, theirs)[0:CHUNK_ROWS, :]
    flat[CHUNK_ROWS:NODE_ROWS, :] = jnp.where(xlo == 0, theirs, mine)[0:CHUNK_ROWS, :]
    new_params[...] = flat[...].astype(jnp.bfloat16)
    factors[...] = factor
    new_master[0:SHARD_ROWS, :] = (
        own_master[0:SHARD_ROWS, :] - learn_rate * own_shard(factors, z) * own_update[0:SHARD_ROWS, :]
    )


def finish(where, tables, own, other, master, update):
    return pl.pallas_call(
        final_kernel,
        in_specs=[pl.BlockSpec(memory_space=pltpu.SMEM)] + [whole()] * 5,
        out_specs=[whole()] * 3,
        out_shape=[
            jax.ShapeDtypeStruct((PIECE, LANES), f32),
            jax.ShapeDtypeStruct((NODE_ROWS, LANES), jnp.bfloat16),
            jax.ShapeDtypeStruct((1, LANES), f32),
        ],
        scratch_shapes=[
            pltpu.VMEM((CHUNK_PAD, LANES), f32),
            pltpu.VMEM((NODE_ROWS, LANES), f32),
            pltpu.VMEM((8 * LAYERS, LANES), f32),
        ],
        compiler_params=params(),
    )(where, tables, own, other, master, update)


def padded(vector):
    return jnp.pad(vector, (0, PIECE * LANES - SHARD)).reshape(PIECE, LANES)


def local(partials, master, first, second, acts, up_cot, out_cot, ln_gain):
    core = lax.axis_index("c")
    layer = lax.axis_index("y") * 2 + lax.axis_index("xh")
    quarter = core * 2 + lax.axis_index("xl")
    swap = ((0, 1), (1, 0))
    core_scalar = core.astype(jnp.int32).reshape(1)
    where = jnp.stack([layer, quarter, lax.axis_index("z")]).astype(jnp.int32)

    grid = partials.reshape(NODES // 2, 2, NODE_ROWS, LANES)
    sent = lax.dynamic_index_in_dim(grid, 1 - core, axis=1, keepdims=False)
    other = lax.ppermute(sent, "c", swap)
    parts, center_rows, inverse_rows = token_sums(acts, up_cot, out_cot)
    parts_other = lax.ppermute(parts, "c", swap)
    chunks = pair_sum(core_scalar, grid, other, parts, parts_other)
    input_grad = input_gradient(acts, up_cot, out_cot, ln_gain, center_rows, inverse_rows)
    chunks = chunks.reshape(NODES, CHUNK_PAD, LANES).astype(f16)

    master, first, second = padded(master), padded(first), padded(second)
    high = master.astype(f16)
    low = ((master - high.astype(f32)) * LOW_SCALE).astype(f16)
    states = [v[0:SHARD_ROWS, :] for v in (first.astype(f16), second.astype(f16), high, low)]
    states = jnp.concatenate(states, axis=0)
    chunks, states, master, first, second, where = lax.optimization_barrier(
        (chunks, states, master, first, second, where)
    )
    blocks = lax.all_to_all(chunks, ("y", "xh", "xl"), 0, 0, tiled=True)
    plane = jnp.sum(blocks.astype(f32), axis=0).astype(f16)
    plane, input_grad = lax.optimization_barrier((plane, input_grad))
    message = jnp.concatenate([plane, states], axis=0)
    message = jnp.broadcast_to(message[None], (8,) + message.shape)
    pieces = lax.all_to_all(message, "z", 0, 0, tiled=True)
    total = jnp.sum(pieces[:, :CHUNK_PAD].astype(f32), axis=0)
    states = pieces[:, CHUNK_PAD:].astype(f32)
    new_first, new_second, stepped, table, update = step(where, total, states, first, second)
    other = lax.ppermute(stepped, "xl", swap)
    tables = lax.all_to_all(table, ("y", "xh", "c", "xl"), 0, 0, tiled=True)
    new_master, new_params, trust = finish(where, tables, stepped, other, master, update)

    def flat(piece):
        return piece.reshape(PIECE * LANES)[:SHARD]

    return (
        flat(new_master),
        flat(new_first),
        flat(new_second),
        new_params.reshape(NODE_PART),
        trust.reshape(LANES)[: 8 * LAYERS],
        input_grad,
    )


def solution(mesh):
    fine = Mesh(mesh.devices.reshape(4, 2, 2, 2, 8), ("y", "xh", "c", "xl", "z"))
    every = ("y", "xh", "c", "xl", "z")
    in_specs = (P(every, None), P(every), P(every), P(every), P(every, None), P(every, None), P(every, None), P())
    out_specs = (P(every), P(every), P(every), P(("y", "xh", "c")), P(), P(every, None))
    return jax.shard_map(local, mesh=fine, in_specs=in_specs, out_specs=out_specs, check_vma=False)
```

```python
import jax
import jax.numpy as jnp
from jax import lax
from jax.experimental import pallas as pl
from jax.experimental.pallas import tpu as pltpu
from jax.sharding import Mesh, PartitionSpec as P

D = 6144
FF = 24576
LAYERS = 8
LENGTH = 9 * D + FF
PARAMS = LAYERS * LENGTH
LANES = 128
NODES = 16
LOCALS = 16
SHARD = PARAMS // (NODES * LOCALS)
NODE_PART = PARAMS // NODES
NODE_ROWS = NODE_PART // LANES
QUARTER_ROWS = NODE_ROWS // 2
PAIR_ROWS = 2 * SHARD // LANES
SHARD_ROWS = 20
PIECE = 24
GROUP = 4
GROUP_ROWS = GROUP * SHARD_ROWS
QUARTER = LENGTH // 4
BOUNDS = (0, D, 2 * D, 5 * D, 6 * D, 7 * D, 8 * D, 8 * D + FF, LENGTH)

beta_one = 0.9
beta_two = 0.999
adam_epsilon = 1e-06
norm_epsilon = 1e-05
learn_rate = 0.01

f32 = jnp.float32
f16 = jnp.float16
SCALE = 128.0
PARTS_SCALE = 1.0 / 64.0
LOW_SCALE = 2048.0
TOKENS_STEP = 32
COLS = D // LANES
VMEM_LIMIT = 16 * 1024 * 1024


def whole():
    return pl.BlockSpec(memory_space=pltpu.VMEM)


def held(x):
    return pltpu.with_memory_space_constraint(x, pltpu.VMEM)


def away(x):
    return pltpu.with_memory_space_constraint(x, pltpu.HBM)


def params():
    return pltpu.CompilerParams(vmem_limit_bytes=VMEM_LIMIT)


def cols(j):
    return slice(j * LANES, (j + 1) * LANES)


def wide(column):
    return jnp.broadcast_to(column, (column.shape[0], LANES))


def norm_kernel(acts, up, out, gain, grad, parts, acts_buf, up_buf, out_buf, grad_buf, sums, sems, grad_sems):
    steps = acts.shape[0] // TOKENS_STEP

    def rows_of(i):
        return pl.ds(pl.multiple_of(i * TOKENS_STEP, TOKENS_STEP), TOKENS_STEP)

    def loads(i):
        rows = rows_of(i)
        pairs = ((acts, acts_buf), (up, up_buf), (out, out_buf))
        return [pltpu.make_async_copy(a.at[rows], b.at[rows], sems.at[k, i]) for k, (a, b) in enumerate(pairs)]

    def store(i):
        rows = rows_of(i)
        return pltpu.make_async_copy(grad_buf.at[rows], grad.at[rows], grad_sems.at[i])

    for i in range(steps):
        for copy in loads(i):
            copy.start()
    sums[...] = jnp.zeros_like(sums)

    def fold(v):
        return jnp.sum(v.reshape(TOKENS_STEP // 8, 8, LANES), axis=0)

    def body(i, carry):
        rows = rows_of(i)
        for copy in loads(i):
            copy.wait()
        total = jnp.zeros((TOKENS_STEP, LANES), f32)
        for j in range(COLS):
            total = total + acts_buf[rows, cols(j)].astype(f32)
        center = wide(jnp.sum(total, axis=1, keepdims=True) * (1.0 / D))
        squares = jnp.zeros((TOKENS_STEP, LANES), f32)
        scaled = jnp.zeros((TOKENS_STEP, LANES), f32)
        cross = jnp.zeros((TOKENS_STEP, LANES), f32)
        for j in range(COLS):
            x = acts_buf[rows, cols(j)].astype(f32) - center
            s = up_buf[rows, cols(j)].astype(f32) * gain[:, cols(j)].astype(f32)
            squares = squares + x * x
            scaled = scaled + s
            cross = cross + s * x
        variance = jnp.sum(squares, axis=1, keepdims=True) * (1.0 / D)
        inverse_col = lax.rsqrt(variance + norm_epsilon)
        inverse = wide(inverse_col)
        mean_scaled = wide(jnp.sum(scaled, axis=1, keepdims=True) * (1.0 / D))
        mean_cross = wide(jnp.sum(cross, axis=1, keepdims=True) * (1.0 / D) * inverse_col)
        for j in range(COLS):
            normed = (acts_buf[rows, cols(j)].astype(f32) - center) * inverse
            u = up_buf[rows, cols(j)].astype(f32)
            o = out_buf[rows, cols(j)].astype(f32)
            inner = u * gain[:, cols(j)].astype(f32) - mean_scaled - normed * mean_cross
            grad_buf[rows, cols(j)] = (o + inverse * inner).astype(jnp.bfloat16)
            sums[0, :, cols(j)] += fold(u * normed)
            sums[1, :, cols(j)] += fold(u)
            sums[2, :, cols(j)] += fold(o)
        store(i).start()
        return carry

    lax.fori_loop(0, steps, body, 0)
    for which in range(3):
        for j in range(COLS):
            row = which * COLS + j
            parts[row : row + 1, :] = jnp.sum(sums[which, :, cols(j)], axis=0, keepdims=True)
    for i in range(steps):
        store(i).wait()


def norm_backward(acts, up, out, gain):
    tokens = acts.shape[0]
    steps = tokens // TOKENS_STEP
    hbm = pl.BlockSpec(memory_space=pltpu.HBM)
    return pl.pallas_call(
        norm_kernel,
        in_specs=[hbm, hbm, hbm, whole()],
        out_specs=[hbm, whole()],
        out_shape=[
            jax.ShapeDtypeStruct((tokens, D), jnp.bfloat16),
            pltpu.VMEM((3 * COLS, LANES), f32),
        ],
        scratch_shapes=[pltpu.VMEM((tokens, D), jnp.bfloat16)] * 4
        + [
            pltpu.VMEM((3, 8, D), f32),
            pltpu.SemaphoreType.DMA((3, steps)),
            pltpu.SemaphoreType.DMA((steps,)),
        ],
        compiler_params=params(),
        cost_estimate=pl.CostEstimate(flops=30 * tokens * D, bytes_accessed=8 * tokens * D, transcendentals=0),
    )(away(acts), away(up), away(out), gain.reshape(1, D))


def lane_index(rows):
    return lax.broadcasted_iota(jnp.int32, (rows, LANES), 1)


def half_kernel(core, grid, half, sems):
    copies = [
        pltpu.make_async_copy(grid.at[i, 1 - core[0]], half.at[i], sems.at[i]) for i in range(NODES // 2)
    ]
    for copy in copies:
        copy.start()
    for copy in copies:
        copy.wait()


def other_half(core, grid):
    return pl.pallas_call(
        half_kernel,
        in_specs=[pl.BlockSpec(memory_space=pltpu.SMEM), pl.BlockSpec(memory_space=pltpu.HBM)],
        out_specs=whole(),
        out_shape=pltpu.VMEM((NODES // 2, NODE_ROWS, LANES), f32),
        scratch_shapes=[pltpu.SemaphoreType.DMA((NODES // 2,))],
        compiler_params=params(),
    )(core, away(grid))


def pair_kernel(core, grid, other, parts, parts_other, result, total, sems):
    count = NODES // 2
    last = count - 1

    def load(i):
        return pltpu.make_async_copy(grid.at[i, core[0]], total.at[i, 0:NODE_ROWS], sems.at[i])

    for i in range(count):
        load(i).start()
    high = lane_index(SHARD_ROWS) >= LANES // 2

    def add(i):
        load(i).wait()
        total[i, 0:NODE_ROWS, :] = (total[i, 0:NODE_ROWS, :] + other[i]) * SCALE
        total[i, NODE_ROWS : NODE_ROWS + 8, :] = jnp.zeros((8, LANES), f32)

    def pack(i):
        for xl in range(2):
            for z in range(8):
                base = QUARTER_ROWS * xl + PAIR_ROWS * (z // 2)
                if z % 2 == 0:
                    piece = total[i, base : base + SHARD_ROWS, :]
                else:
                    first = base + PAIR_ROWS // 2
                    ahead = total[i, first : first + SHARD_ROWS, :]
                    behind = total[i, first + 1 : first + 1 + SHARD_ROWS, :]
                    piece = pltpu.roll(jnp.where(high, ahead, behind), LANES // 2, 1)
                row = SHARD_ROWS * (z // 2)
                result[i, 2 * xl + z % 2, row : row + SHARD_ROWS, :] = piece

    def body(i, carry):
        add(i)
        pack(i)
        return carry

    lax.fori_loop(0, last, body, 0)
    add(last)

    def join(row, first, count):
        added = parts[first : first + count, :] + parts_other[first : first + count, :]
        sums = total[last, row : row + count, :] * (1.0 / SCALE)
        total[last, row : row + count, :] = (sums + added) * PARTS_SCALE

    @pl.when(core[0] == 0)
    def _():
        join(NODE_ROWS - COLS // 2, 0, COLS // 2)

    @pl.when(core[0] == 1)
    def _():
        join(0, COLS // 2, 3 * COLS // 2)
        join(NODE_ROWS - COLS, 2 * COLS, COLS)

    pack(last)


def pair_sum(core, grid, other, parts, parts_other):
    return pl.pallas_call(
        pair_kernel,
        in_specs=[pl.BlockSpec(memory_space=pltpu.SMEM), pl.BlockSpec(memory_space=pltpu.HBM)] + [whole()] * 3,
        out_specs=whole(),
        out_shape=pltpu.VMEM((NODES // 2, 4, GROUP_ROWS, LANES), f32),
        scratch_shapes=[
            pltpu.VMEM((NODES // 2, NODE_ROWS + 8, LANES), f32),
            pltpu.SemaphoreType.DMA((NODES // 2,)),
        ],
        compiler_params=params(),
    )(core, away(grid), held(other), held(parts), held(parts_other))


def place():
    return lax.broadcasted_iota(jnp.int32, (SHARD_ROWS, LANES), 0) * LANES + lane_index(SHARD_ROWS)


def bounds_of(quarter):
    edges = BOUNDS + (LENGTH,)
    result = []
    for j in range(4):
        edge = jnp.int32(edges[j])
        for q in range(1, 4):
            edge = jnp.where(quarter == q, edges[2 * q + j] - q * QUARTER, edge)
        result.append(edge)
    return result


def moments(first, second, grad):
    new_first = beta_one * first + (1.0 - beta_one) * grad
    new_second = beta_two * second + (1.0 - beta_two) * grad * grad
    return new_first, new_second, new_first / (jnp.sqrt(new_second) + adam_epsilon)


def step_kernel(where, total, states, own_first, own_second, new_first, new_second, sent, table, own_update, grads):
    layer, quarter, zh, zb = where[0], where[1], where[2], where[3]
    edges = bounds_of(quarter)
    inside = place()
    valid = inside < SHARD
    weights = [jnp.zeros((SHARD_ROWS, LANES), f32) for _ in range(3)]
    updates = [jnp.zeros((SHARD_ROWS, LANES), f32) for _ in range(3)]
    for i in range(GROUP):
        rows = slice(SHARD_ROWS * i, SHARD_ROWS * (i + 1))
        offset = inside + (2 * i + zb) * SHARD
        place_in_layer = offset + quarter * QUARTER
        added = ((place_in_layer >= BOUNDS[4]) & (place_in_layer < BOUNDS[6])) | (place_in_layer >= BOUNDS[7])
        added = added & (layer == LAYERS - 1)
        grad = total[rows, :] * jnp.where(added, 1.0 / PARTS_SCALE, 1.0 / SCALE)
        grads[i, 0:SHARD_ROWS, :] = grad
        first, second, high, low = (states[i, SHARD_ROWS * k : SHARD_ROWS * (k + 1), :] for k in range(4))
        update = moments(first, second, grad)[2]
        held = high + low * (1.0 / LOW_SCALE)
        sent[0, rows, :] = update
        sent[1, rows, :] = held
        for value, sums in ((held, weights), (update, updates)):
            square = jnp.where(valid, value * value, 0.0)
            for j in range(3):
                mask = (offset >= edges[j]) & (offset < edges[j + 1])
                sums[j] = sums[j] + jnp.where(mask, square, 0.0)
    lane = lane_index(1)
    row = jnp.zeros((1, LANES), f32)
    for base, sums in ((0, weights), (8, updates)):
        for j in range(3):
            column = jnp.sum(jnp.sum(sums[j], axis=0, keepdims=True), axis=1, keepdims=True)
            row = row + jnp.where(lane == base + 2 * quarter + j, column, 0.0)
    table[...] = jnp.broadcast_to(row, (64, LANES))
    first, second, update = moments(
        own_first[0:SHARD_ROWS, :], own_second[0:SHARD_ROWS, :], grads[zh, 0:SHARD_ROWS, :]
    )
    new_first[0:SHARD_ROWS, :] = first
    new_second[0:SHARD_ROWS, :] = second
    own_update[0:SHARD_ROWS, :] = update


def step(where, total, states, first, second):
    shard = jax.ShapeDtypeStruct((PIECE, LANES), f32)
    return pl.pallas_call(
        step_kernel,
        in_specs=[pl.BlockSpec(memory_space=pltpu.SMEM)] + [whole()] * 4,
        out_specs=[whole()] * 5,
        out_shape=[
            shard,
            shard,
            jax.ShapeDtypeStruct((2, GROUP_ROWS, LANES), f32),
            jax.ShapeDtypeStruct((64, LANES), f32),
            shard,
        ],
        scratch_shapes=[pltpu.VMEM((GROUP, PIECE, LANES), f32)],
        compiler_params=params(),
    )(where, total, states, first, second)


def kinds_of(piece):
    found = set()
    for half in range(2):
        low = half * NODE_PART + piece * SHARD
        high = low + SHARD
        found |= {k for k in range(8) if BOUNDS[k] < high and BOUNDS[k + 1] > low}
    return sorted(found)


def final_kernel(where, tables, own, by_xl, by_zb, by_both, master, update, new_master, new_params, trust,
                 gathered, masters, factors, flat, shifted, ratios):
    layer, quarter, zh, zb = where[0], where[1], where[2], where[3]
    core, xl = lax.div(quarter, 2), lax.rem(quarter, 2)
    for n in range(LAYERS):
        table = jnp.sum(tables[8 * n : 8 * n + 8, :], axis=0, keepdims=True)
        ratios[n : n + 1, :] = table
    roots = jnp.sqrt(ratios[...])
    ratio = roots / (pltpu.roll(roots, LANES - 8, 1) + adam_epsilon)
    ratio = jnp.where(lane_index(8) < 8, ratio, 0.0)
    ratios[...] = ratio
    row = jnp.zeros((1, LANES), f32)
    for n in range(LAYERS):
        line = ratios[n : n + 1, :]
        row = row + (pltpu.roll(line, 8 * n, 1) if n else line)
    trust[...] = row
    mine = ratios[pl.ds(layer, 1), :]
    lane = lane_index(1)
    values = [jnp.sum(jnp.where(lane == k, mine, 0.0), axis=1, keepdims=True) for k in range(8)]
    groups = ((own, xl, zb), (by_xl, 1 - xl, zb), (by_zb, xl, 1 - zb), (by_both, 1 - xl, 1 - zb))
    for source, a, b in groups:
        for i in range(GROUP):
            index = 8 * a + 2 * i + b
            for k in range(2):
                gathered[k, index, 0:SHARD_ROWS, :] = source[k, SHARD_ROWS * i : SHARD_ROWS * (i + 1), :]
    start = core * NODE_PART
    inside = place()
    for i in range(LOCALS):
        offset = inside + (start + i * SHARD)
        kinds = kinds_of(i)
        factor = jnp.broadcast_to(values[kinds[0]], (SHARD_ROWS, LANES))
        for k in kinds[1:]:
            factor = jnp.where(offset >= BOUNDS[k], values[k], factor)
        factors[i, 0:SHARD_ROWS, :] = factor
        masters[i, 0:SHARD_ROWS, :] = (
            gathered[1, i, 0:SHARD_ROWS, :] - learn_rate * factor * gathered[0, i, 0:SHARD_ROWS, :]
        )
    index = 8 * xl + 2 * zh + zb
    new_master[0:SHARD_ROWS, :] = (
        master[0:SHARD_ROWS, :] - learn_rate * factors[index, 0:SHARD_ROWS, :] * update[0:SHARD_ROWS, :]
    )
    low = lane_index(SHARD_ROWS) < LANES // 2
    for k in range(LOCALS // 2):
        base = PAIR_ROWS * k
        flat[base : base + 19, :] = masters[2 * k, 0:19, :]
        shifted[0:1, :] = masters[2 * k, 19:20, :]
        shifted[1:21, :] = pltpu.roll(masters[2 * k + 1, 0:SHARD_ROWS, :], LANES // 2, 1)
        flat[base + 19 : base + 39, :] = jnp.where(low, shifted[0:20, :], shifted[1:21, :])
    new_params[...] = flat[...].astype(jnp.bfloat16)


def finish(where, tables, groups, master, update):
    return pl.pallas_call(
        final_kernel,
        in_specs=[pl.BlockSpec(memory_space=pltpu.SMEM)] + [whole()] * 7,
        out_specs=[whole()] * 3,
        out_shape=[
            jax.ShapeDtypeStruct((PIECE, LANES), f32),
            jax.ShapeDtypeStruct((NODE_ROWS, LANES), jnp.bfloat16),
            jax.ShapeDtypeStruct((1, LANES), f32),
        ],
        scratch_shapes=[
            pltpu.VMEM((2, LOCALS, PIECE, LANES), f32),
            pltpu.VMEM((LOCALS, PIECE, LANES), f32),
            pltpu.VMEM((LOCALS, PIECE, LANES), f32),
            pltpu.VMEM((NODE_ROWS, LANES), f32),
            pltpu.VMEM((PIECE, LANES), f32),
            pltpu.VMEM((LAYERS, LANES), f32),
        ],
        compiler_params=params(),
    )(where, tables, *groups, master, update)


def padded(vector):
    return jnp.pad(vector, (0, PIECE * LANES - SHARD)).reshape(PIECE, LANES)


def local(partials, master, first, second, acts, up_cot, out_cot, ln_gain):
    core = lax.axis_index("c")
    layer = lax.axis_index("y") * 2 + lax.axis_index("xh")
    quarter = core * 2 + lax.axis_index("xl")
    swap = ((0, 1), (1, 0))
    core_scalar = core.astype(jnp.int32).reshape(1)
    where = jnp.stack([layer, quarter, lax.axis_index("zh"), lax.axis_index("zb")]).astype(jnp.int32)

    grid = partials.reshape(NODES // 2, 2, NODE_ROWS, LANES)
    sent = other_half(core_scalar, grid)
    other = lax.ppermute(sent, "c", swap)
    input_grad, parts = norm_backward(acts, up_cot, out_cot, ln_gain)
    parts_other = lax.ppermute(parts, "c", swap)
    chunks = pair_sum(core_scalar, grid, other, parts, parts_other)
    chunks = chunks.reshape(32, GROUP_ROWS, LANES).astype(f16)

    master, first, second = padded(master), padded(first), padded(second)
    high = master.astype(f16)
    low = ((master - high.astype(f32)) * LOW_SCALE).astype(f16)
    states = [v[0:SHARD_ROWS, :] for v in (first.astype(f16), second.astype(f16), high, low)]
    states = jnp.concatenate(states, axis=0)
    chunks, states, master, first, second, where = lax.optimization_barrier(
        (chunks, states, master, first, second, where)
    )
    blocks = lax.all_to_all(chunks, ("y", "xh", "xl", "zb"), 0, 0, tiled=True)
    plane = jnp.sum(blocks.astype(f32), axis=0).astype(f16)
    message = jnp.concatenate([plane, states], axis=0)
    message = jnp.broadcast_to(message[None], (GROUP,) + message.shape)
    pieces = lax.all_to_all(message, "zh", 0, 0, tiled=True)
    total = jnp.sum(pieces[:, :GROUP_ROWS].astype(f32), axis=0)
    states = pieces[:, GROUP_ROWS:].astype(f32)
    new_first, new_second, stepped, table, update = step(where, total, states, first, second)
    groups = [
        stepped,
        lax.ppermute(stepped, "xl", swap),
        lax.ppermute(stepped, "zb", swap),
        lax.ppermute(stepped, ("xl", "zb"), ((0, 3), (3, 0), (1, 2), (2, 1))),
    ]
    tables = lax.all_to_all(table.reshape(64, 1, LANES), ("y", "xh", "c", "xl", "zb"), 0, 0, tiled=True)
    new_master, new_params, trust = finish(where, tables.reshape(64, LANES), groups, master, update)

    def flat(piece):
        return piece.reshape(PIECE * LANES)[:SHARD]

    return (
        flat(new_master),
        flat(new_first),
        flat(new_second),
        new_params.reshape(NODE_PART),
        trust.reshape(LANES)[: 8 * LAYERS],
        input_grad,
    )


def solution(mesh):
    every = ("y", "xh", "c", "xl", "zh", "zb")
    fine = Mesh(mesh.devices.reshape(4, 2, 2, 2, 4, 2), every)
    in_specs = (P(every, None), P(every), P(every), P(every), P(every, None), P(every, None), P(every, None), P())
    out_specs = (P(every), P(every), P(every), P(("y", "xh", "c")), P(), P(every, None))
    return jax.shard_map(local, mesh=fine, in_specs=in_specs, out_specs=out_specs, check_vma=False)
```

```python
import jax
import jax.numpy as jnp
from jax import lax
from jax.experimental import pallas as pl
from jax.experimental.pallas import tpu as pltpu
from jax.sharding import Mesh, PartitionSpec as P

D = 6144
FF = 24576
LAYERS = 8
LENGTH = 9 * D + FF
PARAMS = LAYERS * LENGTH
LANES = 128
NODES = 16
LOCALS = 16
SHARD = PARAMS // (NODES * LOCALS)
NODE_PART = PARAMS // NODES
NODE_ROWS = NODE_PART // LANES
QUARTER_ROWS = NODE_ROWS // 2
PAIR_ROWS = 2 * SHARD // LANES
SHARD_ROWS = 20
PIECE = 24
GROUP = 4
GROUP_ROWS = GROUP * SHARD_ROWS
QUARTER = LENGTH // 4
BOUNDS = (0, D, 2 * D, 5 * D, 6 * D, 7 * D, 8 * D, 8 * D + FF, LENGTH)

beta_one = 0.9
beta_two = 0.999
adam_epsilon = 1e-06
norm_epsilon = 1e-05
learn_rate = 0.01

f32 = jnp.float32
f16 = jnp.float16
SCALE = 128.0
PARTS_SCALE = 1.0 / 64.0
LOW_SCALE = 2048.0
TOKENS_STEP = 32
COLS = D // LANES
VMEM_LIMIT = 16 * 1024 * 1024


def whole():
    return pl.BlockSpec(memory_space=pltpu.VMEM)


def held(x):
    return pltpu.with_memory_space_constraint(x, pltpu.VMEM)


def away(x):
    return pltpu.with_memory_space_constraint(x, pltpu.HBM)


def params():
    return pltpu.CompilerParams(vmem_limit_bytes=VMEM_LIMIT)


def cols(j):
    return slice(j * LANES, (j + 1) * LANES)


def wide(column):
    return jnp.broadcast_to(column, (column.shape[0], LANES))


def parts_kernel(acts, up, out, grid, parts, center_rows, inverse_rows, own,
                 acts_buf, up_buf, out_buf, sums, sems, own_sems):
    core = lax.axis_index("c")
    own_copies = [
        pltpu.make_async_copy(grid.at[i, core], own.at[i], own_sems.at[i]) for i in range(NODES // 2)
    ]
    steps = acts.shape[0] // TOKENS_STEP

    def rows_of(i):
        return pl.ds(pl.multiple_of(i * TOKENS_STEP, TOKENS_STEP), TOKENS_STEP)

    def loads(i):
        rows = rows_of(i)
        pairs = ((acts, acts_buf), (up, up_buf), (out, out_buf))
        return [pltpu.make_async_copy(a.at[rows], b.at[rows], sems.at[k, i]) for k, (a, b) in enumerate(pairs)]

    for i in range(steps):
        for copy in loads(i):
            copy.start()
    for copy in own_copies:
        copy.start()
    sums[...] = jnp.zeros_like(sums)

    def fold(v):
        return jnp.sum(v.reshape(TOKENS_STEP // 8, 8, LANES), axis=0)

    def body(i, carry):
        rows = rows_of(i)
        for copy in loads(i):
            copy.wait()
        total = jnp.zeros((TOKENS_STEP, LANES), f32)
        for j in range(COLS):
            total = total + acts_buf[rows, cols(j)].astype(f32)
        center = wide(jnp.sum(total, axis=1, keepdims=True) * (1.0 / D))
        squares = jnp.zeros((TOKENS_STEP, LANES), f32)
        for j in range(COLS):
            x = acts_buf[rows, cols(j)].astype(f32) - center
            squares = squares + x * x
        variance = jnp.sum(squares, axis=1, keepdims=True) * (1.0 / D)
        inverse = wide(lax.rsqrt(variance + norm_epsilon))
        center_rows[rows, :] = center
        inverse_rows[rows, :] = inverse
        for j in range(COLS):
            normed = (acts_buf[rows, cols(j)].astype(f32) - center) * inverse
            u = up_buf[rows, cols(j)].astype(f32)
            sums[0, :, cols(j)] += fold(u * normed)
            sums[1, :, cols(j)] += fold(u)
            sums[2, :, cols(j)] += fold(out_buf[rows, cols(j)].astype(f32))
        return carry

    lax.fori_loop(0, steps, body, 0)
    for which in range(3):
        for j in range(COLS):
            row = which * COLS + j
            parts[row : row + 1, :] = jnp.sum(sums[which, :, cols(j)], axis=0, keepdims=True)
    for copy in own_copies:
        copy.wait()


def token_sums(acts, up, out, grid):
    tokens = acts.shape[0]
    hbm = pl.BlockSpec(memory_space=pltpu.HBM)
    return pl.pallas_call(
        parts_kernel,
        in_specs=[hbm] * 4,
        out_specs=[whole()] * 4,
        out_shape=[
            pltpu.VMEM((3 * COLS, LANES), f32),
            jax.ShapeDtypeStruct((tokens, LANES), f32),
            jax.ShapeDtypeStruct((tokens, LANES), f32),
            pltpu.VMEM((NODES // 2, NODE_ROWS, LANES), f32),
        ],
        scratch_shapes=[pltpu.VMEM((tokens, D), jnp.bfloat16)] * 3
        + [pltpu.VMEM((3, 8, D), f32), pltpu.SemaphoreType.DMA((3, tokens // TOKENS_STEP)), pltpu.SemaphoreType.DMA((NODES // 2,))],
        compiler_params=params(),
        cost_estimate=pl.CostEstimate(flops=15 * tokens * D, bytes_accessed=6 * tokens * D, transcendentals=0),
    )(away(acts), away(up), away(out), away(grid))


def grad_kernel(acts, up, out, gain, center_rows, inverse_rows, grad):
    rows = acts.shape[0]
    center = center_rows[...]
    inverse = inverse_rows[...]
    scaled = jnp.zeros((rows, LANES), f32)
    cross = jnp.zeros((rows, LANES), f32)
    for j in range(COLS):
        s = up[:, cols(j)].astype(f32) * gain[:, cols(j)].astype(f32)
        scaled = scaled + s
        cross = cross + s * (acts[:, cols(j)].astype(f32) - center)
    mean_scaled = wide(jnp.sum(scaled, axis=1, keepdims=True) * (1.0 / D))
    mean_cross = wide(jnp.sum(cross, axis=1, keepdims=True) * (1.0 / D)) * inverse
    for j in range(COLS):
        normed = (acts[:, cols(j)].astype(f32) - center) * inverse
        s = up[:, cols(j)].astype(f32) * gain[:, cols(j)].astype(f32)
        inner = s - mean_scaled - normed * mean_cross
        grad[:, cols(j)] = (out[:, cols(j)].astype(f32) + inverse * inner).astype(jnp.bfloat16)


def input_gradient(acts, up, out, gain, center_rows, inverse_rows):
    tokens = acts.shape[0]
    block = pl.BlockSpec((TOKENS_STEP, D), lambda i: (i, 0))
    rows = pl.BlockSpec((TOKENS_STEP, LANES), lambda i: (i, 0))
    return pl.pallas_call(
        grad_kernel,
        grid=(tokens // TOKENS_STEP,),
        in_specs=[block, block, block, pl.BlockSpec((1, D), lambda i: (0, 0)), rows, rows],
        out_specs=block,
        out_shape=jax.ShapeDtypeStruct((tokens, D), jnp.bfloat16),
        compiler_params=params(),
        cost_estimate=pl.CostEstimate(flops=15 * tokens * D, bytes_accessed=8 * tokens * D, transcendentals=0),
    )(away(acts), away(up), away(out), gain.reshape(1, D), center_rows, inverse_rows)


def lane_index(rows):
    return lax.broadcasted_iota(jnp.int32, (rows, LANES), 1)


def position():
    layer = lax.axis_index("y") * 2 + lax.axis_index("xh")
    return layer, lax.axis_index("c"), lax.axis_index("xl"), lax.axis_index("zh"), lax.axis_index("zb")


def half_kernel(grid, half, sems):
    core = lax.axis_index("c")
    copies = [
        pltpu.make_async_copy(grid.at[i, 1 - core], half.at[i], sems.at[i]) for i in range(NODES // 2)
    ]
    for copy in copies:
        copy.start()
    for copy in copies:
        copy.wait()


def other_half(grid):
    return pl.pallas_call(
        half_kernel,
        in_specs=[pl.BlockSpec(memory_space=pltpu.HBM)],
        out_specs=whole(),
        out_shape=pltpu.VMEM((NODES // 2, NODE_ROWS, LANES), f32),
        scratch_shapes=[pltpu.SemaphoreType.DMA((NODES // 2,))],
        compiler_params=params(),
    )(away(grid))


def pair_kernel(own, other, parts, parts_other, result, total):
    core = lax.axis_index("c")
    count = NODES // 2
    last = count - 1
    high = lane_index(SHARD_ROWS) >= LANES // 2

    def add(i):
        total[0:NODE_ROWS, :] = (own[i] + other[i]) * SCALE
        total[NODE_ROWS : NODE_ROWS + 8, :] = jnp.zeros((8, LANES), f32)

    def pack(i):
        for xl in range(2):
            for z in range(8):
                base = QUARTER_ROWS * xl + PAIR_ROWS * (z // 2)
                if z % 2 == 0:
                    piece = total[base : base + SHARD_ROWS, :]
                else:
                    first = base + PAIR_ROWS // 2
                    ahead = total[first : first + SHARD_ROWS, :]
                    behind = total[first + 1 : first + 1 + SHARD_ROWS, :]
                    piece = pltpu.roll(jnp.where(high, ahead, behind), LANES // 2, 1)
                row = SHARD_ROWS * (z // 2)
                result[i, 2 * xl + z % 2, row : row + SHARD_ROWS, :] = piece

    def body(i, carry):
        add(i)
        pack(i)
        return carry

    lax.fori_loop(0, last, body, 0)
    add(last)

    def join(row, first, count):
        added = parts[first : first + count, :] + parts_other[first : first + count, :]
        sums = own[last, row : row + count, :] + other[last, row : row + count, :]
        total[row : row + count, :] = (sums + added) * PARTS_SCALE

    @pl.when(core == 0)
    def _():
        join(NODE_ROWS - COLS // 2, 0, COLS // 2)

    @pl.when(core == 1)
    def _():
        join(0, COLS // 2, 3 * COLS // 2)
        join(NODE_ROWS - COLS, 2 * COLS, COLS)

    pack(last)


def pair_sum(own, other, parts, parts_other):
    return pl.pallas_call(
        pair_kernel,
        in_specs=[whole()] * 4,
        out_specs=whole(),
        out_shape=pltpu.VMEM((NODES // 2, 4, GROUP_ROWS, LANES), f32),
        scratch_shapes=[pltpu.VMEM((NODE_ROWS + 8, LANES), f32)],
        compiler_params=params(),
    )(held(own), held(other), held(parts), held(parts_other))


def place(rows):
    return lax.broadcasted_iota(jnp.int32, (rows, LANES), 0) * LANES + lane_index(rows)


def bounds_of(quarter):
    edges = BOUNDS + (LENGTH,)
    result = []
    for j in range(4):
        edge = jnp.int32(edges[j])
        for q in range(1, 4):
            edge = jnp.where(quarter == q, edges[2 * q + j] - q * QUARTER, edge)
        result.append(edge)
    return result


def moments(first, second, grad):
    new_first = beta_one * first + (1.0 - beta_one) * grad
    new_second = beta_two * second + (1.0 - beta_two) * grad * grad
    return new_first, new_second, new_first / (jnp.sqrt(new_second) + adam_epsilon)


def step_kernel(total, states, own_first, own_second, new_first, new_second, sent, table, own_update, grads):
    layer, core, xl, zh, zb = position()
    quarter = 2 * core + xl
    edges = bounds_of(quarter)
    inside = place(SHARD_ROWS)
    valid = inside < SHARD
    weights = [jnp.zeros((SHARD_ROWS, LANES), f32) for _ in range(3)]
    updates = [jnp.zeros((SHARD_ROWS, LANES), f32) for _ in range(3)]
    for i in range(GROUP):
        rows = slice(SHARD_ROWS * i, SHARD_ROWS * (i + 1))
        offset = inside + (2 * i + zb) * SHARD
        place_in_layer = offset + quarter * QUARTER
        added = ((place_in_layer >= BOUNDS[4]) & (place_in_layer < BOUNDS[6])) | (place_in_layer >= BOUNDS[7])
        added = added & (layer == LAYERS - 1)
        grad = total[rows, :] * jnp.where(added, 1.0 / PARTS_SCALE, 1.0 / SCALE)
        grads[i, 0:SHARD_ROWS, :] = grad
        first, second, high, low = (states[i, SHARD_ROWS * k : SHARD_ROWS * (k + 1), :] for k in range(4))
        update = moments(first, second, grad)[2]
        held = high + low * (1.0 / LOW_SCALE)
        sent[0, rows, :] = update
        sent[1, rows, :] = held
        for value, sums in ((held, weights), (update, updates)):
            square = jnp.where(valid, value * value, 0.0)
            for j in range(3):
                mask = (offset >= edges[j]) & (offset < edges[j + 1])
                sums[j] = sums[j] + jnp.where(mask, square, 0.0)
    lane = lane_index(1)
    row = jnp.zeros((1, LANES), f32)
    for base, sums in ((0, weights), (8, updates)):
        for j in range(3):
            column = jnp.sum(jnp.sum(sums[j], axis=0, keepdims=True), axis=1, keepdims=True)
            row = row + jnp.where(lane == base + 2 * quarter + j, column, 0.0)
    table[...] = jnp.broadcast_to(row, (64, LANES))
    first, second, update = moments(
        own_first[0:SHARD_ROWS, :], own_second[0:SHARD_ROWS, :], grads[zh, 0:SHARD_ROWS, :]
    )
    new_first[0:SHARD_ROWS, :] = first
    new_second[0:SHARD_ROWS, :] = second
    own_update[0:SHARD_ROWS, :] = update


def step(total, states, first, second):
    shard = jax.ShapeDtypeStruct((PIECE, LANES), f32)
    return pl.pallas_call(
        step_kernel,
        in_specs=[whole()] * 4,
        out_specs=[whole()] * 5,
        out_shape=[
            shard,
            shard,
            jax.ShapeDtypeStruct((2, GROUP_ROWS, LANES), f32),
            jax.ShapeDtypeStruct((64, LANES), f32),
            shard,
        ],
        scratch_shapes=[pltpu.VMEM((GROUP, PIECE, LANES), f32)],
        compiler_params=params(),
    )(total, states, first, second)


def layout_kernel(own, by_xl, by_zb, by_both, updates, masters, gathered, shifted):
    xl, zb = lax.axis_index("xl"), lax.axis_index("zb")
    groups = ((own, xl, zb), (by_xl, 1 - xl, zb), (by_zb, xl, 1 - zb), (by_both, 1 - xl, 1 - zb))
    low = lane_index(SHARD_ROWS) < LANES // 2
    for k, flat in enumerate((updates, masters)):
        for source, a, b in groups:
            for i in range(GROUP):
                rows = slice(SHARD_ROWS * i, SHARD_ROWS * (i + 1))
                gathered[8 * a + 2 * i + b, 0:SHARD_ROWS, :] = source[k, rows, :]
        for i in range(LOCALS // 2):
            base = PAIR_ROWS * i
            flat[base : base + 19, :] = gathered[2 * i, 0:19, :]
            shifted[0:1, :] = gathered[2 * i, 19:20, :]
            shifted[1:21, :] = pltpu.roll(gathered[2 * i + 1, 0:SHARD_ROWS, :], LANES // 2, 1)
            flat[base + 19 : base + 39, :] = jnp.where(low, shifted[0:20, :], shifted[1:21, :])


def layout(groups):
    return pl.pallas_call(
        layout_kernel,
        in_specs=[whole()] * 4,
        out_specs=[whole()] * 2,
        out_shape=[pltpu.VMEM((NODE_ROWS, LANES), f32)] * 2,
        scratch_shapes=[pltpu.VMEM((LOCALS, PIECE, LANES), f32), pltpu.VMEM((PIECE, LANES), f32)],
        compiler_params=params(),
    )(*groups)


def final_kernel(tables, updates, masters, master, update, new_master, new_params, trust, ratios):
    layer, core, xl, zh, zb = position()
    for n in range(LAYERS):
        ratios[n : n + 1, :] = jnp.sum(tables[8 * n : 8 * n + 8, :], axis=0, keepdims=True)
    roots = jnp.sqrt(ratios[...])
    ratio = roots / (pltpu.roll(roots, LANES - 8, 1) + adam_epsilon)
    ratio = jnp.where(lane_index(8) < 8, ratio, 0.0)
    ratios[...] = ratio
    row = jnp.zeros((1, LANES), f32)
    for n in range(LAYERS):
        line = ratios[n : n + 1, :]
        row = row + (pltpu.roll(line, 8 * n, 1) if n else line)
    trust[...] = row[:, 0 : 8 * LAYERS]
    mine = ratios[pl.ds(layer, 1), :]
    lane = lane_index(1)
    values = [jnp.sum(jnp.where(lane == k, mine, 0.0), axis=1, keepdims=True) for k in range(8)]

    def spread(offset):
        factor = jnp.broadcast_to(values[0], offset.shape)
        for k in range(1, 8):
            factor = jnp.where(offset >= BOUNDS[k], values[k], factor)
        return factor

    start = core * NODE_PART
    index = 8 * xl + 2 * zh + zb
    new_master[0:SHARD_ROWS, :] = (
        master[0:SHARD_ROWS, :]
        - learn_rate * spread(place(SHARD_ROWS) + (start + index * SHARD)) * update[0:SHARD_ROWS, :]
    )
    step_rows = 104
    for i in range(NODE_ROWS // step_rows):
        rows = slice(step_rows * i, step_rows * (i + 1))
        factor = spread(place(step_rows) + (start + i * step_rows * LANES))
        new_params[rows, :] = (masters[rows, :] - learn_rate * factor * updates[rows, :]).astype(jnp.bfloat16)


def finish(tables, updates, masters, master, update):
    return pl.pallas_call(
        final_kernel,
        in_specs=[whole()] * 5,
        out_specs=[whole()] * 3,
        out_shape=[
            jax.ShapeDtypeStruct((PIECE, LANES), f32),
            jax.ShapeDtypeStruct((NODE_ROWS, LANES), jnp.bfloat16),
            jax.ShapeDtypeStruct((1, 8 * LAYERS), f32),
        ],
        scratch_shapes=[pltpu.VMEM((LAYERS, LANES), f32)],
        compiler_params=params(),
    )(tables, updates, masters, master, update)


def padded(vector):
    return jnp.pad(vector, (0, PIECE * LANES - SHARD)).reshape(PIECE, LANES)


def local(partials, master, first, second, acts, up_cot, out_cot, ln_gain):
    swap = ((0, 1), (1, 0))
    grid = partials.reshape(NODES // 2, 2, NODE_ROWS, LANES)
    sent = other_half(grid)
    other = lax.ppermute(sent, "c", swap)
    parts, center_rows, inverse_rows, own = token_sums(acts, up_cot, out_cot, grid)
    parts_other = lax.ppermute(parts, "c", swap)
    chunks = pair_sum(own, other, parts, parts_other)
    chunks = chunks.reshape(32, GROUP_ROWS, LANES).astype(f16)

    master, first, second = padded(master), padded(first), padded(second)
    high = master.astype(f16)
    low = ((master - high.astype(f32)) * LOW_SCALE).astype(f16)
    states = [v[0:SHARD_ROWS, :] for v in (first.astype(f16), second.astype(f16), high, low)]
    states = jnp.concatenate(states, axis=0)
    chunks, states, master, first, second = lax.optimization_barrier((chunks, states, master, first, second))
    blocks = lax.all_to_all(chunks, ("y", "xh", "xl", "zb"), 0, 0, tiled=True)
    plane = jnp.sum(blocks.astype(f32), axis=0).astype(f16)
    message = jnp.concatenate([plane, states], axis=0)
    message = jnp.broadcast_to(message[None], (GROUP,) + message.shape)
    pieces = lax.all_to_all(message, "zh", 0, 0, tiled=True)
    total = jnp.sum(pieces[:, :GROUP_ROWS].astype(f32), axis=0)
    states = pieces[:, GROUP_ROWS:].astype(f32)
    new_first, new_second, stepped, table, update = step(total, states, first, second)
    table, center_rows, inverse_rows = lax.optimization_barrier((table, center_rows, inverse_rows))
    input_grad = input_gradient(acts, up_cot, out_cot, ln_gain, center_rows, inverse_rows)
    groups = [
        stepped,
        lax.ppermute(stepped, "xl", swap),
        lax.ppermute(stepped, "zb", swap),
        lax.ppermute(stepped, ("xl", "zb"), ((0, 3), (3, 0), (1, 2), (2, 1))),
    ]
    tables = lax.all_to_all(table.reshape(64, 1, LANES), ("y", "xh", "c", "xl", "zb"), 0, 0, tiled=True)
    updates, masters = layout(groups)
    new_master, new_params, trust = finish(tables.reshape(64, LANES), updates, masters, master, update)

    def flat(piece):
        return piece.reshape(PIECE * LANES)[:SHARD]

    return (
        flat(new_master),
        flat(new_first),
        flat(new_second),
        new_params.reshape(NODE_PART),
        trust.reshape(8 * LAYERS),
        input_grad,
    )


def solution(mesh):
    every = ("y", "xh", "c", "xl", "zh", "zb")
    fine = Mesh(mesh.devices.reshape(4, 2, 2, 2, 4, 2), every)
    in_specs = (P(every, None), P(every), P(every), P(every), P(every, None), P(every, None), P(every, None), P())
    out_specs = (P(every), P(every), P(every), P(("y", "xh", "c")), P(), P(every, None))
    return jax.shard_map(local, mesh=fine, in_specs=in_specs, out_specs=out_specs, check_vma=False)
```

```python
import jax
import jax.numpy as jnp
from jax import lax
from jax.experimental import pallas as pl
from jax.experimental.pallas import tpu as pltpu
from jax.sharding import Mesh, PartitionSpec as P

D = 6144
FF = 24576
LAYERS = 8
LENGTH = 9 * D + FF
PARAMS = LAYERS * LENGTH
LANES = 128
NODES = 16
LOCALS = 16
SHARD = PARAMS // (NODES * LOCALS)
NODE_PART = PARAMS // NODES
NODE_ROWS = NODE_PART // LANES
QUARTER_ROWS = NODE_ROWS // 2
PAIR_ROWS = 2 * SHARD // LANES
SHARD_ROWS = 20
PIECE = 24
GROUP = 4
GROUP_ROWS = GROUP * SHARD_ROWS
QUARTER = LENGTH // 4
BOUNDS = (0, D, 2 * D, 5 * D, 6 * D, 7 * D, 8 * D, 8 * D + FF, LENGTH)

beta_one = 0.9
beta_two = 0.999
adam_epsilon = 1e-06
norm_epsilon = 1e-05
learn_rate = 0.01

f32 = jnp.float32
f16 = jnp.float16
SCALE = 128.0
PARTS_SCALE = 1.0 / 64.0
LOW_SCALE = 2048.0
TOKENS_STEP = 32
SUMS_STEP = 64
COLS = D // LANES
VMEM_LIMIT = 16 * 1024 * 1024


def whole():
    return pl.BlockSpec(memory_space=pltpu.VMEM)


def held(x):
    return pltpu.with_memory_space_constraint(x, pltpu.VMEM)


def away(x):
    return pltpu.with_memory_space_constraint(x, pltpu.HBM)


def params():
    return pltpu.CompilerParams(vmem_limit_bytes=VMEM_LIMIT)


def cols(j):
    return slice(j * LANES, (j + 1) * LANES)


def wide(column):
    return jnp.broadcast_to(column, (column.shape[0], LANES))


def parts_kernel(acts, up, out, grid, parts, center_rows, inverse_rows, own,
                 up_buf, out_buf, sums, sems, own_sems):
    core = lax.axis_index("c")
    own_copies = [
        pltpu.make_async_copy(grid.at[i, core], own.at[i], own_sems.at[i]) for i in range(NODES // 2)
    ]
    steps = acts.shape[0] // SUMS_STEP

    def rows_of(i):
        return pl.ds(pl.multiple_of(i * SUMS_STEP, SUMS_STEP), SUMS_STEP)

    def loads(i):
        rows = rows_of(i)
        pairs = ((up, up_buf), (out, out_buf))
        return [pltpu.make_async_copy(a.at[rows], b.at[rows], sems.at[k, i]) for k, (a, b) in enumerate(pairs)]

    for i in range(steps):
        for copy in loads(i):
            copy.start()
    for copy in own_copies:
        copy.start()
    sums[...] = jnp.zeros_like(sums)

    def fold(v):
        return jnp.sum(v.reshape(SUMS_STEP // 8, 8, LANES), axis=0)

    def body(i, carry):
        rows = rows_of(i)
        total = jnp.zeros((SUMS_STEP, LANES), f32)
        for j in range(COLS):
            total = total + acts[rows, cols(j)].astype(f32)
        center = wide(jnp.sum(total, axis=1, keepdims=True) * (1.0 / D))
        squares = jnp.zeros((SUMS_STEP, LANES), f32)
        for j in range(COLS):
            x = acts[rows, cols(j)].astype(f32) - center
            squares = squares + x * x
        variance = jnp.sum(squares, axis=1, keepdims=True) * (1.0 / D)
        inverse = wide(lax.rsqrt(variance + norm_epsilon))
        center_rows[rows, :] = center
        inverse_rows[rows, :] = inverse
        for copy in loads(i):
            copy.wait()
        for j in range(COLS):
            normed = (acts[rows, cols(j)].astype(f32) - center) * inverse
            u = up_buf[rows, cols(j)].astype(f32)
            sums[0, :, cols(j)] += fold(u * normed)
            sums[1, :, cols(j)] += fold(u)
            sums[2, :, cols(j)] += fold(out_buf[rows, cols(j)].astype(f32))
        return carry

    lax.fori_loop(0, steps, body, 0)
    for which in range(3):
        for j in range(COLS):
            row = which * COLS + j
            parts[row : row + 1, :] = jnp.sum(sums[which, :, cols(j)], axis=0, keepdims=True)
    for copy in own_copies:
        copy.wait()


def token_sums(acts, up, out, grid):
    tokens = acts.shape[0]
    hbm = pl.BlockSpec(memory_space=pltpu.HBM)
    return pl.pallas_call(
        parts_kernel,
        in_specs=[whole()] + [hbm] * 3,
        out_specs=[whole()] * 4,
        out_shape=[
            pltpu.VMEM((3 * COLS, LANES), f32),
            jax.ShapeDtypeStruct((tokens, LANES), f32),
            jax.ShapeDtypeStruct((tokens, LANES), f32),
            pltpu.VMEM((NODES // 2, NODE_ROWS, LANES), f32),
        ],
        scratch_shapes=[pltpu.VMEM((tokens, D), jnp.bfloat16)] * 2
        + [pltpu.VMEM((3, 8, D), f32), pltpu.SemaphoreType.DMA((2, tokens // SUMS_STEP)), pltpu.SemaphoreType.DMA((NODES // 2,))],
        compiler_params=params(),
        cost_estimate=pl.CostEstimate(flops=15 * tokens * D, bytes_accessed=6 * tokens * D, transcendentals=0),
    )(held(acts), away(up), away(out), away(grid))


def grad_kernel(acts, up, out, gain, center_rows, inverse_rows, grad):
    rows = acts.shape[0]
    center = center_rows[...]
    inverse = inverse_rows[...]
    scaled = jnp.zeros((rows, LANES), f32)
    cross = jnp.zeros((rows, LANES), f32)
    for j in range(COLS):
        s = up[:, cols(j)].astype(f32) * gain[:, cols(j)].astype(f32)
        scaled = scaled + s
        cross = cross + s * (acts[:, cols(j)].astype(f32) - center)
    mean_scaled = wide(jnp.sum(scaled, axis=1, keepdims=True) * (1.0 / D))
    mean_cross = wide(jnp.sum(cross, axis=1, keepdims=True) * (1.0 / D)) * inverse
    for j in range(COLS):
        normed = (acts[:, cols(j)].astype(f32) - center) * inverse
        s = up[:, cols(j)].astype(f32) * gain[:, cols(j)].astype(f32)
        inner = s - mean_scaled - normed * mean_cross
        grad[:, cols(j)] = (out[:, cols(j)].astype(f32) + inverse * inner).astype(jnp.bfloat16)


def input_gradient(acts, up, out, gain, center_rows, inverse_rows):
    tokens = acts.shape[0]
    block = pl.BlockSpec((TOKENS_STEP, D), lambda i: (i, 0))
    rows = pl.BlockSpec((TOKENS_STEP, LANES), lambda i: (i, 0))
    return pl.pallas_call(
        grad_kernel,
        grid=(tokens // TOKENS_STEP,),
        in_specs=[block, block, block, pl.BlockSpec((1, D), lambda i: (0, 0)), rows, rows],
        out_specs=block,
        out_shape=jax.ShapeDtypeStruct((tokens, D), jnp.bfloat16),
        compiler_params=params(),
        cost_estimate=pl.CostEstimate(flops=15 * tokens * D, bytes_accessed=8 * tokens * D, transcendentals=0),
    )(away(acts), away(up), away(out), gain.reshape(1, D), center_rows, inverse_rows)


def lane_index(rows):
    return lax.broadcasted_iota(jnp.int32, (rows, LANES), 1)


def position():
    layer = lax.axis_index("y") * 2 + lax.axis_index("xh")
    return layer, lax.axis_index("c"), lax.axis_index("xl"), lax.axis_index("zh"), lax.axis_index("zb")


def half_kernel(grid, half, sems):
    core = lax.axis_index("c")
    copies = [
        pltpu.make_async_copy(grid.at[i, 1 - core], half.at[i], sems.at[i]) for i in range(NODES // 2)
    ]
    for copy in copies:
        copy.start()
    for copy in copies:
        copy.wait()


def other_half(grid):
    return pl.pallas_call(
        half_kernel,
        in_specs=[pl.BlockSpec(memory_space=pltpu.HBM)],
        out_specs=whole(),
        out_shape=pltpu.VMEM((NODES // 2, NODE_ROWS, LANES), f32),
        scratch_shapes=[pltpu.SemaphoreType.DMA((NODES // 2,))],
        compiler_params=params(),
    )(away(grid))


def pair_kernel(own, other, parts, parts_other, result, total):
    core = lax.axis_index("c")
    count = NODES // 2
    last = count - 1
    high = lane_index(SHARD_ROWS) >= LANES // 2

    def add(i):
        total[0:NODE_ROWS, :] = (own[i] + other[i]) * SCALE
        total[NODE_ROWS : NODE_ROWS + 8, :] = jnp.zeros((8, LANES), f32)

    def pack(i):
        for xl in range(2):
            for z in range(8):
                base = QUARTER_ROWS * xl + PAIR_ROWS * (z // 2)
                if z % 2 == 0:
                    piece = total[base : base + SHARD_ROWS, :]
                else:
                    first = base + PAIR_ROWS // 2
                    ahead = total[first : first + SHARD_ROWS, :]
                    behind = total[first + 1 : first + 1 + SHARD_ROWS, :]
                    piece = pltpu.roll(jnp.where(high, ahead, behind), LANES // 2, 1)
                row = SHARD_ROWS * (z // 2)
                block = lax.rem(i, 2) * 16 + 8 * xl + 4 * (z % 2) + lax.div(i, 2)
                result[block, row : row + SHARD_ROWS, :] = piece

    def body(i, carry):
        add(i)
        pack(i)
        return carry

    lax.fori_loop(0, last, body, 0)
    add(last)

    def join(row, first, count):
        added = parts[first : first + count, :] + parts_other[first : first + count, :]
        sums = own[last, row : row + count, :] + other[last, row : row + count, :]
        total[row : row + count, :] = (sums + added) * PARTS_SCALE

    @pl.when(core == 0)
    def _():
        join(NODE_ROWS - COLS // 2, 0, COLS // 2)

    @pl.when(core == 1)
    def _():
        join(0, COLS // 2, 3 * COLS // 2)
        join(NODE_ROWS - COLS, 2 * COLS, COLS)

    pack(jnp.int32(last))


def pair_sum(own, other, parts, parts_other):
    return pl.pallas_call(
        pair_kernel,
        in_specs=[whole()] * 4,
        out_specs=whole(),
        out_shape=pltpu.VMEM((32, GROUP_ROWS, LANES), f32),
        scratch_shapes=[pltpu.VMEM((NODE_ROWS + 8, LANES), f32)],
        compiler_params=params(),
    )(held(own), held(other), held(parts), held(parts_other))


def place(rows):
    return lax.broadcasted_iota(jnp.int32, (rows, LANES), 0) * LANES + lane_index(rows)


def bounds_of(quarter):
    edges = BOUNDS + (LENGTH,)
    result = []
    for j in range(4):
        edge = jnp.int32(edges[j])
        for q in range(1, 4):
            edge = jnp.where(quarter == q, edges[2 * q + j] - q * QUARTER, edge)
        result.append(edge)
    return result


def moments(first, second, grad):
    new_first = beta_one * first + (1.0 - beta_one) * grad
    new_second = beta_two * second + (1.0 - beta_two) * grad * grad
    return new_first, new_second, new_first / (jnp.sqrt(new_second) + adam_epsilon)


def step_kernel(ours, near, mid, far, own_first, own_second, new_first, new_second, sent, table, own_update,
                grads, pieces):
    layer, core, xl, zh, zb = position()
    quarter = 2 * core + xl
    edges = bounds_of(quarter)
    for k, piece in enumerate((ours, near, mid, far)):
        pieces[k, :, :] = piece[...]
    source = [lax.bitwise_xor(zh, i) for i in range(GROUP)]
    inside = place(SHARD_ROWS)
    valid = inside < SHARD
    weights = [jnp.zeros((SHARD_ROWS, LANES), f32) for _ in range(3)]
    updates = [jnp.zeros((SHARD_ROWS, LANES), f32) for _ in range(3)]
    for i in range(GROUP):
        rows = slice(SHARD_ROWS * i, SHARD_ROWS * (i + 1))
        offset = inside + (2 * i + zb) * SHARD
        place_in_layer = offset + quarter * QUARTER
        added = ((place_in_layer >= BOUNDS[4]) & (place_in_layer < BOUNDS[6])) | (place_in_layer >= BOUNDS[7])
        added = added & (layer == LAYERS - 1)
        total = pieces[source[0], rows, :]
        for k in range(1, GROUP):
            total = total + pieces[source[k], rows, :]
        grad = total * jnp.where(added, 1.0 / PARTS_SCALE, 1.0 / SCALE)
        grads[i, 0:SHARD_ROWS, :] = grad
        first, second, high, low = (
            pieces[source[i], GROUP_ROWS + SHARD_ROWS * k : GROUP_ROWS + SHARD_ROWS * (k + 1), :] for k in range(4)
        )
        update = moments(first, second, grad)[2]
        held = high + low * (1.0 / LOW_SCALE)
        sent[0, rows, :] = update
        sent[1, rows, :] = held
        for value, sums in ((held, weights), (update, updates)):
            square = jnp.where(valid, value * value, 0.0)
            for j in range(3):
                mask = (offset >= edges[j]) & (offset < edges[j + 1])
                sums[j] = sums[j] + jnp.where(mask, square, 0.0)
    lane = lane_index(1)
    row = jnp.zeros((1, LANES), f32)
    for base, sums in ((0, weights), (8, updates)):
        for j in range(3):
            column = jnp.sum(jnp.sum(sums[j], axis=0, keepdims=True), axis=1, keepdims=True)
            row = row + jnp.where(lane == base + 2 * quarter + j, column, 0.0)
    table[...] = jnp.broadcast_to(row, (64, LANES))
    first, second, update = moments(
        own_first[0:SHARD_ROWS, :], own_second[0:SHARD_ROWS, :], grads[zh, 0:SHARD_ROWS, :]
    )
    new_first[0:SHARD_ROWS, :] = first
    new_second[0:SHARD_ROWS, :] = second
    own_update[0:SHARD_ROWS, :] = update


def step(pieces, first, second):
    shard = jax.ShapeDtypeStruct((PIECE, LANES), f32)
    return pl.pallas_call(
        step_kernel,
        in_specs=[whole()] * 6,
        out_specs=[whole()] * 5,
        out_shape=[
            shard,
            shard,
            jax.ShapeDtypeStruct((2, GROUP_ROWS, LANES), f32),
            jax.ShapeDtypeStruct((64, LANES), f32),
            shard,
        ],
        scratch_shapes=[
            pltpu.VMEM((GROUP, PIECE, LANES), f32),
            pltpu.VMEM((GROUP, 2 * GROUP_ROWS, LANES), f32),
        ],
        compiler_params=params(),
    )(*pieces, first, second)


def layout_kernel(own, by_xl, by_zb, by_both, updates, masters, gathered, shifted):
    xl, zb = lax.axis_index("xl"), lax.axis_index("zb")
    groups = ((own, xl, zb), (by_xl, 1 - xl, zb), (by_zb, xl, 1 - zb), (by_both, 1 - xl, 1 - zb))
    low = lane_index(SHARD_ROWS) < LANES // 2
    for k, flat in enumerate((updates, masters)):
        for source, a, b in groups:
            for i in range(GROUP):
                rows = slice(SHARD_ROWS * i, SHARD_ROWS * (i + 1))
                gathered[8 * a + 2 * i + b, 0:SHARD_ROWS, :] = source[k, rows, :]
        for i in range(LOCALS // 2):
            base = PAIR_ROWS * i
            flat[base : base + 19, :] = gathered[2 * i, 0:19, :]
            shifted[0:1, :] = gathered[2 * i, 19:20, :]
            shifted[1:21, :] = pltpu.roll(gathered[2 * i + 1, 0:SHARD_ROWS, :], LANES // 2, 1)
            flat[base + 19 : base + 39, :] = jnp.where(low, shifted[0:20, :], shifted[1:21, :])


def layout(groups):
    return pl.pallas_call(
        layout_kernel,
        in_specs=[whole()] * 4,
        out_specs=[whole()] * 2,
        out_shape=[pltpu.VMEM((NODE_ROWS, LANES), f32)] * 2,
        scratch_shapes=[pltpu.VMEM((LOCALS, PIECE, LANES), f32), pltpu.VMEM((PIECE, LANES), f32)],
        compiler_params=params(),
    )(*groups)


def final_kernel(tables, updates, masters, master, update, new_master, new_params, trust, ratios):
    layer, core, xl, zh, zb = position()
    for n in range(LAYERS):
        ratios[n : n + 1, :] = jnp.sum(tables[8 * n : 8 * n + 8, :], axis=0, keepdims=True)
    roots = jnp.sqrt(ratios[...])
    ratio = roots / (pltpu.roll(roots, LANES - 8, 1) + adam_epsilon)
    ratio = jnp.where(lane_index(8) < 8, ratio, 0.0)
    ratios[...] = ratio
    row = jnp.zeros((1, LANES), f32)
    for n in range(LAYERS):
        line = ratios[n : n + 1, :]
        row = row + (pltpu.roll(line, 8 * n, 1) if n else line)
    trust[...] = row[:, 0 : 8 * LAYERS]
    mine = ratios[pl.ds(layer, 1), :]
    lane = lane_index(1)
    values = [jnp.sum(jnp.where(lane == k, mine, 0.0), axis=1, keepdims=True) for k in range(8)]

    def spread(offset):
        factor = jnp.broadcast_to(values[0], offset.shape)
        for k in range(1, 8):
            factor = jnp.where(offset >= BOUNDS[k], values[k], factor)
        return factor

    start = core * NODE_PART
    index = 8 * xl + 2 * zh + zb
    new_master[0:SHARD_ROWS, :] = (
        master[0:SHARD_ROWS, :]
        - learn_rate * spread(place(SHARD_ROWS) + (start + index * SHARD)) * update[0:SHARD_ROWS, :]
    )
    step_rows = 104
    for i in range(NODE_ROWS // step_rows):
        rows = slice(step_rows * i, step_rows * (i + 1))
        factor = spread(place(step_rows) + (start + i * step_rows * LANES))
        new_params[rows, :] = (masters[rows, :] - learn_rate * factor * updates[rows, :]).astype(jnp.bfloat16)


def finish(tables, updates, masters, master, update):
    return pl.pallas_call(
        final_kernel,
        in_specs=[whole()] * 5,
        out_specs=[whole()] * 3,
        out_shape=[
            jax.ShapeDtypeStruct((PIECE, LANES), f32),
            jax.ShapeDtypeStruct((NODE_ROWS, LANES), jnp.bfloat16),
            jax.ShapeDtypeStruct((1, 8 * LAYERS), f32),
        ],
        scratch_shapes=[pltpu.VMEM((LAYERS, LANES), f32)],
        compiler_params=params(),
    )(tables, updates, masters, master, update)


def padded(vector):
    return jnp.pad(vector, (0, PIECE * LANES - SHARD)).reshape(PIECE, LANES)


def local(partials, master, first, second, acts, up_cot, out_cot, ln_gain):
    swap = ((0, 1), (1, 0))
    grid = partials.reshape(NODES // 2, 2, NODE_ROWS, LANES)
    sent = other_half(grid)
    other = lax.ppermute(sent, "c", swap)
    parts, center_rows, inverse_rows, own = token_sums(acts, up_cot, out_cot, grid)
    parts_other = lax.ppermute(parts, "c", swap)
    chunks = pair_sum(own, other, parts, parts_other)
    chunks = chunks.astype(f16)

    master, first, second = padded(master), padded(first), padded(second)
    high = master.astype(f16)
    low = ((master - high.astype(f32)) * LOW_SCALE).astype(f16)
    states = [v[0:SHARD_ROWS, :] for v in (first.astype(f16), second.astype(f16), high, low)]
    states = jnp.concatenate(states, axis=0)
    chunks, states, master, first, second = lax.optimization_barrier((chunks, states, master, first, second))
    blocks = lax.all_to_all(chunks, ("xh", "xl", "zb", "y"), 0, 0, tiled=True)
    plane = jnp.sum(blocks.astype(f32), axis=0).astype(f16)
    message = jnp.concatenate([plane, states], axis=0)
    pieces = [message] + [lax.ppermute(message, "zh", [(i, i ^ k) for i in range(GROUP)]) for k in (1, 2, 3)]
    pieces = [piece.astype(f32) for piece in pieces]
    new_first, new_second, stepped, table, update = step(pieces, first, second)
    table, center_rows, inverse_rows = lax.optimization_barrier((table, center_rows, inverse_rows))
    input_grad = input_gradient(acts, up_cot, out_cot, ln_gain, center_rows, inverse_rows)
    groups = [
        stepped,
        lax.ppermute(stepped, "xl", swap),
        lax.ppermute(stepped, "zb", swap),
        lax.ppermute(stepped, ("xl", "zb"), ((0, 3), (3, 0), (1, 2), (2, 1))),
    ]
    tables = lax.all_to_all(table.reshape(64, 1, LANES), ("y", "xh", "c", "xl", "zb"), 0, 0, tiled=True)
    updates, masters = layout(groups)
    new_master, new_params, trust = finish(tables.reshape(64, LANES), updates, masters, master, update)

    def flat(piece):
        return piece.reshape(PIECE * LANES)[:SHARD]

    return (
        flat(new_master),
        flat(new_first),
        flat(new_second),
        new_params.reshape(NODE_PART),
        trust.reshape(8 * LAYERS),
        input_grad,
    )


def solution(mesh):
    every = ("y", "xh", "c", "xl", "zh", "zb")
    fine = Mesh(mesh.devices.reshape(4, 2, 2, 2, 4, 2), every)
    in_specs = (P(every, None), P(every), P(every), P(every), P(every, None), P(every, None), P(every, None), P())
    out_specs = (P(every), P(every), P(every), P(("y", "xh", "c")), P(), P(every, None))
    return jax.shard_map(local, mesh=fine, in_specs=in_specs, out_specs=out_specs, check_vma=False)
```

```python
import jax
import jax.numpy as jnp
from jax import lax
from jax.experimental import pallas as pl
from jax.experimental.pallas import tpu as pltpu
from jax.sharding import Mesh, PartitionSpec as P

D = 6144
FF = 24576
LAYERS = 8
LENGTH = 9 * D + FF
PARAMS = LAYERS * LENGTH
LANES = 128
NODES = 16
LOCALS = 16
SHARD = PARAMS // (NODES * LOCALS)
NODE_PART = PARAMS // NODES
NODE_ROWS = NODE_PART // LANES
QUARTER_ROWS = NODE_ROWS // 2
PAIR_ROWS = 2 * SHARD // LANES
SHARD_ROWS = 20
PIECE = 24
GROUP = 4
GROUP_ROWS = GROUP * SHARD_ROWS
QUARTER = LENGTH // 4
BOUNDS = (0, D, 2 * D, 5 * D, 6 * D, 7 * D, 8 * D, 8 * D + FF, LENGTH)

beta_one = 0.9
beta_two = 0.999
adam_epsilon = 1e-06
norm_epsilon = 1e-05
learn_rate = 0.01

f32 = jnp.float32
f16 = jnp.float16
SCALE = 128.0
PARTS_SCALE = 1.0 / 64.0
LOW_SCALE = 2048.0
TOKENS_STEP = 32
SUMS_STEP = 64
COLS = D // LANES
VMEM_LIMIT = 16 * 1024 * 1024


def whole():
    return pl.BlockSpec(memory_space=pltpu.VMEM)


def held(x):
    return pltpu.with_memory_space_constraint(x, pltpu.VMEM)


def away(x):
    return pltpu.with_memory_space_constraint(x, pltpu.HBM)


def params():
    return pltpu.CompilerParams(vmem_limit_bytes=VMEM_LIMIT)


def cols(j):
    return slice(j * LANES, (j + 1) * LANES)


def wide(column):
    return jnp.broadcast_to(column, (column.shape[0], LANES))


def parts_kernel(acts, up, out, grid, parts, center_rows, inverse_rows, own,
                 up_buf, out_buf, sums, sems, own_sems):
    core = lax.axis_index("c")
    own_copies = [
        pltpu.make_async_copy(grid.at[i, core], own.at[i], own_sems.at[i]) for i in range(NODES // 2)
    ]
    steps = acts.shape[0] // SUMS_STEP

    def rows_of(i):
        return pl.ds(pl.multiple_of(i * SUMS_STEP, SUMS_STEP), SUMS_STEP)

    def loads(i):
        rows = rows_of(i)
        pairs = ((up, up_buf), (out, out_buf))
        return [pltpu.make_async_copy(a.at[rows], b.at[rows], sems.at[k, i]) for k, (a, b) in enumerate(pairs)]

    for i in range(steps):
        for copy in loads(i):
            copy.start()
    for copy in own_copies:
        copy.start()
    sums[...] = jnp.zeros_like(sums)

    def fold(v):
        return jnp.sum(v.reshape(SUMS_STEP // 8, 8, LANES), axis=0)

    def body(i, carry):
        rows = rows_of(i)
        total = jnp.zeros((SUMS_STEP, LANES), f32)
        for j in range(COLS):
            total = total + acts[rows, cols(j)].astype(f32)
        center = wide(jnp.sum(total, axis=1, keepdims=True) * (1.0 / D))
        squares = jnp.zeros((SUMS_STEP, LANES), f32)
        for j in range(COLS):
            x = acts[rows, cols(j)].astype(f32) - center
            squares = squares + x * x
        variance = jnp.sum(squares, axis=1, keepdims=True) * (1.0 / D)
        inverse = wide(lax.rsqrt(variance + norm_epsilon))
        center_rows[rows, :] = center
        inverse_rows[rows, :] = inverse
        for copy in loads(i):
            copy.wait()
        for j in range(COLS):
            normed = (acts[rows, cols(j)].astype(f32) - center) * inverse
            u = up_buf[rows, cols(j)].astype(f32)
            sums[0, :, cols(j)] += fold(u * normed)
            sums[1, :, cols(j)] += fold(u)
            sums[2, :, cols(j)] += fold(out_buf[rows, cols(j)].astype(f32))
        return carry

    lax.fori_loop(0, steps, body, 0)
    for which in range(3):
        for j in range(COLS):
            row = which * COLS + j
            parts[row : row + 1, :] = jnp.sum(sums[which, :, cols(j)], axis=0, keepdims=True)
    for copy in own_copies:
        copy.wait()


def token_sums(acts, up, out, grid):
    tokens = acts.shape[0]
    hbm = pl.BlockSpec(memory_space=pltpu.HBM)
    return pl.pallas_call(
        parts_kernel,
        in_specs=[whole()] + [hbm] * 3,
        out_specs=[whole()] * 4,
        out_shape=[
            pltpu.VMEM((3 * COLS, LANES), f32),
            jax.ShapeDtypeStruct((tokens, LANES), f32),
            jax.ShapeDtypeStruct((tokens, LANES), f32),
            pltpu.VMEM((NODES // 2, NODE_ROWS, LANES), f32),
        ],
        scratch_shapes=[pltpu.VMEM((tokens, D), jnp.bfloat16)] * 2
        + [pltpu.VMEM((3, 8, D), f32), pltpu.SemaphoreType.DMA((2, tokens // SUMS_STEP)), pltpu.SemaphoreType.DMA((NODES // 2,))],
        compiler_params=params(),
        cost_estimate=pl.CostEstimate(flops=15 * tokens * D, bytes_accessed=6 * tokens * D, transcendentals=0),
    )(held(acts), away(up), away(out), away(grid))


def grad_kernel(acts_hbm, up_hbm, out_hbm, gain, center_rows, inverse_rows, grad,
                acts, up, out, grad_buf, load_sems, sems):
    steps = acts.shape[0] // TOKENS_STEP

    def rows_of(i):
        return pl.ds(pl.multiple_of(i * TOKENS_STEP, TOKENS_STEP), TOKENS_STEP)

    def loads(i):
        rows = rows_of(i)
        pairs = ((acts_hbm, acts), (up_hbm, up), (out_hbm, out))
        return [pltpu.make_async_copy(a.at[rows], b.at[rows], load_sems.at[k, i]) for k, (a, b) in enumerate(pairs)]

    def store(i):
        rows = rows_of(i)
        return pltpu.make_async_copy(grad_buf.at[rows], grad.at[rows], sems.at[i])

    for i in range(steps):
        for copy in loads(i):
            copy.start()

    def body(i, carry):
        rows = rows_of(i)
        for copy in loads(i):
            copy.wait()
        center = center_rows[rows, :]
        inverse = inverse_rows[rows, :]
        scaled = jnp.zeros((TOKENS_STEP, LANES), f32)
        cross = jnp.zeros((TOKENS_STEP, LANES), f32)
        for j in range(COLS):
            s = up[rows, cols(j)].astype(f32) * gain[:, cols(j)].astype(f32)
            scaled = scaled + s
            cross = cross + s * (acts[rows, cols(j)].astype(f32) - center)
        mean_scaled = wide(jnp.sum(scaled, axis=1, keepdims=True) * (1.0 / D))
        mean_cross = wide(jnp.sum(cross, axis=1, keepdims=True) * (1.0 / D)) * inverse
        for j in range(COLS):
            normed = (acts[rows, cols(j)].astype(f32) - center) * inverse
            s = up[rows, cols(j)].astype(f32) * gain[:, cols(j)].astype(f32)
            inner = s - mean_scaled - normed * mean_cross
            grad_buf[rows, cols(j)] = (out[rows, cols(j)].astype(f32) + inverse * inner).astype(jnp.bfloat16)
        store(i).start()
        return carry

    lax.fori_loop(0, steps, body, 0)
    for i in range(steps):
        store(i).wait()


def input_gradient(acts, up, out, gain, center_rows, inverse_rows):
    tokens = acts.shape[0]
    return pl.pallas_call(
        grad_kernel,
        in_specs=[pl.BlockSpec(memory_space=pltpu.HBM)] * 3 + [whole()] * 3,
        out_specs=pl.BlockSpec(memory_space=pltpu.HBM),
        out_shape=jax.ShapeDtypeStruct((tokens, D), jnp.bfloat16),
        scratch_shapes=[pltpu.VMEM((tokens, D), jnp.bfloat16)] * 4
        + [
            pltpu.SemaphoreType.DMA((3, tokens // TOKENS_STEP)),
            pltpu.SemaphoreType.DMA((tokens // TOKENS_STEP,)),
        ],
        compiler_params=params(),
        cost_estimate=pl.CostEstimate(flops=15 * tokens * D, bytes_accessed=8 * tokens * D, transcendentals=0),
    )(away(acts), away(up), away(out), gain.reshape(1, D), center_rows, inverse_rows)


def lane_index(rows):
    return lax.broadcasted_iota(jnp.int32, (rows, LANES), 1)


def position():
    layer = lax.axis_index("y") * 2 + lax.axis_index("xh")
    return layer, lax.axis_index("c"), lax.axis_index("xl"), lax.axis_index("zh"), lax.axis_index("zb")


def half_kernel(grid, half, sems):
    core = lax.axis_index("c")
    copies = [
        pltpu.make_async_copy(grid.at[i, 1 - core], half.at[i], sems.at[i]) for i in range(NODES // 2)
    ]
    for copy in copies:
        copy.start()
    for copy in copies:
        copy.wait()


def other_half(grid):
    return pl.pallas_call(
        half_kernel,
        in_specs=[pl.BlockSpec(memory_space=pltpu.HBM)],
        out_specs=whole(),
        out_shape=pltpu.VMEM((NODES // 2, NODE_ROWS, LANES), f32),
        scratch_shapes=[pltpu.SemaphoreType.DMA((NODES // 2,))],
        compiler_params=params(),
    )(away(grid))


def pair_kernel(own, other, parts, parts_other, result, total):
    core = lax.axis_index("c")
    count = NODES // 2
    last = count - 1
    high = lane_index(SHARD_ROWS) >= LANES // 2

    def add(i):
        total[0:NODE_ROWS, :] = (own[i] + other[i]) * SCALE
        total[NODE_ROWS : NODE_ROWS + 8, :] = jnp.zeros((8, LANES), f32)

    def pack(i):
        for xl in range(2):
            for z in range(8):
                base = QUARTER_ROWS * xl + PAIR_ROWS * (z // 2)
                if z % 2 == 0:
                    piece = total[base : base + SHARD_ROWS, :]
                else:
                    first = base + PAIR_ROWS // 2
                    ahead = total[first : first + SHARD_ROWS, :]
                    behind = total[first + 1 : first + 1 + SHARD_ROWS, :]
                    piece = pltpu.roll(jnp.where(high, ahead, behind), LANES // 2, 1)
                row = SHARD_ROWS * (z // 2)
                block = lax.rem(i, 2) * 16 + 8 * xl + 4 * (z % 2) + lax.div(i, 2)
                result[block, row : row + SHARD_ROWS, :] = piece

    def body(i, carry):
        add(i)
        pack(i)
        return carry

    lax.fori_loop(0, last, body, 0)
    add(last)

    def join(row, first, count):
        added = parts[first : first + count, :] + parts_other[first : first + count, :]
        sums = own[last, row : row + count, :] + other[last, row : row + count, :]
        total[row : row + count, :] = (sums + added) * PARTS_SCALE

    @pl.when(core == 0)
    def _():
        join(NODE_ROWS - COLS // 2, 0, COLS // 2)

    @pl.when(core == 1)
    def _():
        join(0, COLS // 2, 3 * COLS // 2)
        join(NODE_ROWS - COLS, 2 * COLS, COLS)

    pack(jnp.int32(last))


def pair_sum(own, other, parts, parts_other):
    return pl.pallas_call(
        pair_kernel,
        in_specs=[whole()] * 4,
        out_specs=whole(),
        out_shape=pltpu.VMEM((32, GROUP_ROWS, LANES), f32),
        scratch_shapes=[pltpu.VMEM((NODE_ROWS + 8, LANES), f32)],
        compiler_params=params(),
    )(held(own), held(other), held(parts), held(parts_other))


def place(rows):
    return lax.broadcasted_iota(jnp.int32, (rows, LANES), 0) * LANES + lane_index(rows)


def bounds_of(quarter):
    edges = BOUNDS + (LENGTH,)
    result = []
    for j in range(4):
        edge = jnp.int32(edges[j])
        for q in range(1, 4):
            edge = jnp.where(quarter == q, edges[2 * q + j] - q * QUARTER, edge)
        result.append(edge)
    return result


def moments(first, second, grad):
    new_first = beta_one * first + (1.0 - beta_one) * grad
    new_second = beta_two * second + (1.0 - beta_two) * grad * grad
    return new_first, new_second, new_first / (jnp.sqrt(new_second) + adam_epsilon)


def step_kernel(far, ours, ahead, behind, own_first, own_second, new_first, new_second, sent, table, own_update,
                grads, pieces):
    layer, core, xl, zh, zb = position()
    quarter = 2 * core + xl
    edges = bounds_of(quarter)
    for k, piece in enumerate((ours, ahead, far, behind)):
        pieces[k, :, :] = piece[...]
    source = [lax.rem(i + GROUP - zh, GROUP) for i in range(GROUP)]
    inside = place(SHARD_ROWS)
    valid = inside < SHARD
    weights = [jnp.zeros((SHARD_ROWS, LANES), f32) for _ in range(3)]
    updates = [jnp.zeros((SHARD_ROWS, LANES), f32) for _ in range(3)]
    for i in range(GROUP):
        rows = slice(SHARD_ROWS * i, SHARD_ROWS * (i + 1))
        offset = inside + (2 * i + zb) * SHARD
        place_in_layer = offset + quarter * QUARTER
        added = ((place_in_layer >= BOUNDS[4]) & (place_in_layer < BOUNDS[6])) | (place_in_layer >= BOUNDS[7])
        added = added & (layer == LAYERS - 1)
        total = pieces[source[0], rows, :]
        for k in range(1, GROUP):
            total = total + pieces[source[k], rows, :]
        grad = total * jnp.where(added, 1.0 / PARTS_SCALE, 1.0 / SCALE)
        grads[i, 0:SHARD_ROWS, :] = grad
        first, second, high, low = (
            pieces[source[i], GROUP_ROWS + SHARD_ROWS * k : GROUP_ROWS + SHARD_ROWS * (k + 1), :] for k in range(4)
        )
        update = moments(first, second, grad)[2]
        held = high + low * (1.0 / LOW_SCALE)
        sent[0, rows, :] = update
        sent[1, rows, :] = held
        for value, sums in ((held, weights), (update, updates)):
            square = jnp.where(valid, value * value, 0.0)
            for j in range(3):
                mask = (offset >= edges[j]) & (offset < edges[j + 1])
                sums[j] = sums[j] + jnp.where(mask, square, 0.0)
    lane = lane_index(1)
    row = jnp.zeros((1, LANES), f32)
    for base, sums in ((0, weights), (8, updates)):
        for j in range(3):
            column = jnp.sum(jnp.sum(sums[j], axis=0, keepdims=True), axis=1, keepdims=True)
            row = row + jnp.where(lane == base + 2 * quarter + j, column, 0.0)
    table[...] = jnp.broadcast_to(row, (64, LANES))
    first, second, update = moments(
        own_first[0:SHARD_ROWS, :], own_second[0:SHARD_ROWS, :], grads[zh, 0:SHARD_ROWS, :]
    )
    new_first[0:SHARD_ROWS, :] = first
    new_second[0:SHARD_ROWS, :] = second
    own_update[0:SHARD_ROWS, :] = update


def step(pieces, first, second):
    shard = jax.ShapeDtypeStruct((PIECE, LANES), f32)
    return pl.pallas_call(
        step_kernel,
        in_specs=[whole()] * 6,
        out_specs=[whole()] * 5,
        out_shape=[
            shard,
            shard,
            jax.ShapeDtypeStruct((2, GROUP_ROWS, LANES), f32),
            jax.ShapeDtypeStruct((64, LANES), f32),
            shard,
        ],
        scratch_shapes=[
            pltpu.VMEM((GROUP, PIECE, LANES), f32),
            pltpu.VMEM((GROUP, 2 * GROUP_ROWS, LANES), f32),
        ],
        compiler_params=params(),
    )(*pieces, first, second)


def layout_kernel(own, by_xl, by_zb, by_both, updates, masters, gathered, shifted):
    xl, zb = lax.axis_index("xl"), lax.axis_index("zb")
    groups = ((own, xl, zb), (by_xl, 1 - xl, zb), (by_zb, xl, 1 - zb), (by_both, 1 - xl, 1 - zb))
    low = lane_index(SHARD_ROWS) < LANES // 2
    for k, flat in enumerate((updates, masters)):
        for source, a, b in groups:
            for i in range(GROUP):
                rows = slice(SHARD_ROWS * i, SHARD_ROWS * (i + 1))
                gathered[8 * a + 2 * i + b, 0:SHARD_ROWS, :] = source[k, rows, :]
        for i in range(LOCALS // 2):
            base = PAIR_ROWS * i
            flat[base : base + 19, :] = gathered[2 * i, 0:19, :]
            shifted[0:1, :] = gathered[2 * i, 19:20, :]
            shifted[1:21, :] = pltpu.roll(gathered[2 * i + 1, 0:SHARD_ROWS, :], LANES // 2, 1)
            flat[base + 19 : base + 39, :] = jnp.where(low, shifted[0:20, :], shifted[1:21, :])


def layout(groups):
    return pl.pallas_call(
        layout_kernel,
        in_specs=[whole()] * 4,
        out_specs=[whole()] * 2,
        out_shape=[pltpu.VMEM((NODE_ROWS, LANES), f32)] * 2,
        scratch_shapes=[pltpu.VMEM((LOCALS, PIECE, LANES), f32), pltpu.VMEM((PIECE, LANES), f32)],
        compiler_params=params(),
    )(*groups)


def final_kernel(tables, updates, masters, master, update, new_master, new_params, trust, ratios):
    layer, core, xl, zh, zb = position()
    sums = tables[0:LAYERS, :]
    for n in range(1, 8):
        sums = sums + tables[LAYERS * n : LAYERS * (n + 1), :]
    roots = jnp.sqrt(sums)
    ratio = roots / (pltpu.roll(roots, LANES - 8, 1) + adam_epsilon)
    ratio = jnp.where(lane_index(8) < 8, ratio, 0.0)
    ratios[...] = ratio
    row = jnp.zeros((1, LANES), f32)
    for n in range(LAYERS):
        line = ratios[n : n + 1, :]
        row = row + (pltpu.roll(line, 8 * n, 1) if n else line)
    trust[...] = row[:, 0 : 8 * LAYERS]
    mine = ratios[pl.ds(layer, 1), :]
    lane = lane_index(1)
    values = [jnp.sum(jnp.where(lane == k, mine, 0.0), axis=1, keepdims=True) for k in range(8)]

    def spread(offset):
        factor = jnp.broadcast_to(values[0], offset.shape)
        for k in range(1, 8):
            factor = jnp.where(offset >= BOUNDS[k], values[k], factor)
        return factor

    start = core * NODE_PART
    index = 8 * xl + 2 * zh + zb
    new_master[0:SHARD_ROWS, :] = (
        master[0:SHARD_ROWS, :]
        - learn_rate * spread(place(SHARD_ROWS) + (start + index * SHARD)) * update[0:SHARD_ROWS, :]
    )
    step_rows = 104
    for i in range(NODE_ROWS // step_rows):
        rows = slice(step_rows * i, step_rows * (i + 1))
        factor = spread(place(step_rows) + (start + i * step_rows * LANES))
        new_params[rows, :] = (masters[rows, :] - learn_rate * factor * updates[rows, :]).astype(jnp.bfloat16)


def finish(tables, updates, masters, master, update):
    return pl.pallas_call(
        final_kernel,
        in_specs=[whole()] * 5,
        out_specs=[whole()] * 3,
        out_shape=[
            jax.ShapeDtypeStruct((PIECE, LANES), f32),
            jax.ShapeDtypeStruct((NODE_ROWS, LANES), jnp.bfloat16),
            jax.ShapeDtypeStruct((1, 8 * LAYERS), f32),
        ],
        scratch_shapes=[pltpu.VMEM((LAYERS, LANES), f32)],
        compiler_params=params(),
    )(tables, updates, masters, master, update)


def padded(vector):
    return jnp.pad(vector, (0, PIECE * LANES - SHARD)).reshape(PIECE, LANES)


def local(partials, master, first, second, acts, up_cot, out_cot, ln_gain):
    swap = ((0, 1), (1, 0))
    grid = partials.reshape(NODES // 2, 2, NODE_ROWS, LANES)
    sent = other_half(grid)
    other = lax.ppermute(sent, "c", swap)
    parts, center_rows, inverse_rows, own = token_sums(acts, up_cot, out_cot, grid)
    parts_other = lax.ppermute(parts, "c", swap)
    chunks = pair_sum(own, other, parts, parts_other)
    chunks = chunks.astype(f16)

    master, first, second = padded(master), padded(first), padded(second)
    high = master.astype(f16)
    low = ((master - high.astype(f32)) * LOW_SCALE).astype(f16)
    states = [v[0:SHARD_ROWS, :] for v in (first.astype(f16), second.astype(f16), high, low)]
    states = jnp.concatenate(states, axis=0)
    chunks, states, master, first, second = lax.optimization_barrier((chunks, states, master, first, second))
    blocks = lax.all_to_all(chunks, ("xh", "xl", "zb", "y"), 0, 0, tiled=True)
    plane = jnp.sum(blocks.astype(f32), axis=0).astype(f16)
    message = jnp.concatenate([plane, states], axis=0)
    far = lax.ppermute(message, "zh", [(i, i ^ 2) for i in range(GROUP)])
    near = [lax.ppermute(message, "zh", [(i, (i + k) % GROUP) for i in range(GROUP)]) for k in (1, 3)]
    pieces = [far, message, near[1], near[0]]
    pieces = [piece.astype(f32) for piece in pieces]
    new_first, new_second, stepped, table, update = step(pieces, first, second)
    table, center_rows, inverse_rows = lax.optimization_barrier((table, center_rows, inverse_rows))
    input_grad = input_gradient(acts, up_cot, out_cot, ln_gain, center_rows, inverse_rows)
    groups = [
        stepped,
        lax.ppermute(stepped, "xl", swap),
        lax.ppermute(stepped, "zb", swap),
        lax.ppermute(stepped, ("xl", "zb"), ((0, 3), (3, 0), (1, 2), (2, 1))),
    ]
    tables = lax.all_to_all(table.reshape(64, 1, LANES), ("c", "xl", "zb", "y", "xh"), 0, 0, tiled=True)
    updates, masters = layout(groups)
    new_master, new_params, trust = finish(tables.reshape(64, LANES), updates, masters, master, update)

    def flat(piece):
        return piece.reshape(PIECE * LANES)[:SHARD]

    return (
        flat(new_master),
        flat(new_first),
        flat(new_second),
        new_params.reshape(NODE_PART),
        trust.reshape(8 * LAYERS),
        input_grad,
    )


def solution(mesh):
    every = ("y", "xh", "c", "xl", "zh", "zb")
    fine = Mesh(mesh.devices.reshape(4, 2, 2, 2, 4, 2), every)
    in_specs = (P(every, None), P(every), P(every), P(every), P(every, None), P(every, None), P(every, None), P())
    out_specs = (P(every), P(every), P(every), P(("y", "xh", "c")), P(), P(every, None))
    return jax.shard_map(local, mesh=fine, in_specs=in_specs, out_specs=out_specs, check_vma=False)
```

```python
import jax
import jax.numpy as jnp
from jax import lax
from jax.experimental import pallas as pl
from jax.experimental.pallas import tpu as pltpu
from jax.sharding import Mesh, PartitionSpec as P

D = 6144
FF = 24576
LAYERS = 8
LENGTH = 9 * D + FF
PARAMS = LAYERS * LENGTH
LANES = 128
NODES = 16
LOCALS = 16
SHARD = PARAMS // (NODES * LOCALS)
NODE_PART = PARAMS // NODES
NODE_ROWS = NODE_PART // LANES
QUARTER_ROWS = NODE_ROWS // 2
PAIR_ROWS = 2 * SHARD // LANES
SHARD_ROWS = 20
PIECE = 24
GROUP = 4
GROUP_ROWS = GROUP * SHARD_ROWS
QUARTER = LENGTH // 4
BOUNDS = (0, D, 2 * D, 5 * D, 6 * D, 7 * D, 8 * D, 8 * D + FF, LENGTH)

beta_one = 0.9
beta_two = 0.999
adam_epsilon = 1e-06
norm_epsilon = 1e-05
learn_rate = 0.01

f32 = jnp.float32
f16 = jnp.float16
SCALE = 128.0
PARTS_SCALE = 1.0 / 64.0
LOW_SCALE = 2048.0
TOKENS_STEP = 32
SUMS_STEP = 64
COLS = D // LANES
VMEM_LIMIT = 16 * 1024 * 1024


def whole():
    return pl.BlockSpec(memory_space=pltpu.VMEM)


def held(x):
    return pltpu.with_memory_space_constraint(x, pltpu.VMEM)


def away(x):
    return pltpu.with_memory_space_constraint(x, pltpu.HBM)


def params():
    return pltpu.CompilerParams(vmem_limit_bytes=VMEM_LIMIT)


def cols(j):
    return slice(j * LANES, (j + 1) * LANES)


def wide(column):
    return jnp.broadcast_to(column, (column.shape[0], LANES))


def parts_kernel(acts, up, out, grid, parts, center_rows, inverse_rows, own,
                 up_buf, out_buf, sums, sems, own_sems):
    core = lax.axis_index("c")
    own_copies = [
        pltpu.make_async_copy(grid.at[i, core], own.at[i], own_sems.at[i]) for i in range(NODES // 2)
    ]
    steps = acts.shape[0] // SUMS_STEP

    def rows_of(i):
        return pl.ds(pl.multiple_of(i * SUMS_STEP, SUMS_STEP), SUMS_STEP)

    def loads(i):
        rows = rows_of(i)
        pairs = ((up, up_buf), (out, out_buf))
        return [pltpu.make_async_copy(a.at[rows], b.at[rows], sems.at[k, i]) for k, (a, b) in enumerate(pairs)]

    for i in range(steps):
        for copy in loads(i):
            copy.start()
    for copy in own_copies:
        copy.start()
    sums[...] = jnp.zeros_like(sums)

    def fold(v):
        return jnp.sum(v.reshape(SUMS_STEP // 8, 8, LANES), axis=0)

    def body(i, carry):
        rows = rows_of(i)
        total = jnp.zeros((SUMS_STEP, LANES), f32)
        for j in range(COLS):
            total = total + acts[rows, cols(j)].astype(f32)
        center = wide(jnp.sum(total, axis=1, keepdims=True) * (1.0 / D))
        squares = jnp.zeros((SUMS_STEP, LANES), f32)
        for j in range(COLS):
            x = acts[rows, cols(j)].astype(f32) - center
            squares = squares + x * x
        variance = jnp.sum(squares, axis=1, keepdims=True) * (1.0 / D)
        inverse = wide(lax.rsqrt(variance + norm_epsilon))
        center_rows[rows, :] = center
        inverse_rows[rows, :] = inverse
        for copy in loads(i):
            copy.wait()
        for j in range(COLS):
            normed = (acts[rows, cols(j)].astype(f32) - center) * inverse
            u = up_buf[rows, cols(j)].astype(f32)
            sums[0, :, cols(j)] += fold(u * normed)
            sums[1, :, cols(j)] += fold(u)
            sums[2, :, cols(j)] += fold(out_buf[rows, cols(j)].astype(f32))
        return carry

    lax.fori_loop(0, steps, body, 0)
    for which in range(3):
        for j in range(COLS):
            row = which * COLS + j
            parts[row : row + 1, :] = jnp.sum(sums[which, :, cols(j)], axis=0, keepdims=True)
    for copy in own_copies:
        copy.wait()


def token_sums(acts, up, out, grid):
    tokens = acts.shape[0]
    hbm = pl.BlockSpec(memory_space=pltpu.HBM)
    return pl.pallas_call(
        parts_kernel,
        in_specs=[whole()] + [hbm] * 3,
        out_specs=[whole()] * 4,
        out_shape=[
            pltpu.VMEM((3 * COLS, LANES), f32),
            jax.ShapeDtypeStruct((tokens, LANES), f32),
            jax.ShapeDtypeStruct((tokens, LANES), f32),
            pltpu.VMEM((NODES // 2, NODE_ROWS, LANES), f32),
        ],
        scratch_shapes=[pltpu.VMEM((tokens, D), jnp.bfloat16)] * 2
        + [pltpu.VMEM((3, 8, D), f32), pltpu.SemaphoreType.DMA((2, tokens // SUMS_STEP)), pltpu.SemaphoreType.DMA((NODES // 2,))],
        compiler_params=params(),
        cost_estimate=pl.CostEstimate(flops=15 * tokens * D, bytes_accessed=6 * tokens * D, transcendentals=0),
    )(held(acts), away(up), away(out), away(grid))


def grad_kernel(acts_hbm, up_hbm, out_hbm, gain, center_rows, inverse_rows, grad,
                acts, up, out, grad_buf, load_sems, sems):
    steps = acts.shape[0] // TOKENS_STEP

    def rows_of(i):
        return pl.ds(pl.multiple_of(i * TOKENS_STEP, TOKENS_STEP), TOKENS_STEP)

    def loads(i):
        rows = rows_of(i)
        pairs = ((acts_hbm, acts), (up_hbm, up), (out_hbm, out))
        return [pltpu.make_async_copy(a.at[rows], b.at[rows], load_sems.at[k, i]) for k, (a, b) in enumerate(pairs)]

    def store(i):
        rows = rows_of(i)
        return pltpu.make_async_copy(grad_buf.at[rows], grad.at[rows], sems.at[i])

    for i in range(steps):
        for copy in loads(i):
            copy.start()

    def body(i, carry):
        rows = rows_of(i)
        for copy in loads(i):
            copy.wait()
        center = center_rows[rows, :]
        inverse = inverse_rows[rows, :]
        scaled = jnp.zeros((TOKENS_STEP, LANES), f32)
        cross = jnp.zeros((TOKENS_STEP, LANES), f32)
        for j in range(COLS):
            s = up[rows, cols(j)].astype(f32) * gain[:, cols(j)].astype(f32)
            scaled = scaled + s
            cross = cross + s * (acts[rows, cols(j)].astype(f32) - center)
        mean_scaled = wide(jnp.sum(scaled, axis=1, keepdims=True) * (1.0 / D))
        mean_cross = wide(jnp.sum(cross, axis=1, keepdims=True) * (1.0 / D)) * inverse
        for j in range(COLS):
            normed = (acts[rows, cols(j)].astype(f32) - center) * inverse
            s = up[rows, cols(j)].astype(f32) * gain[:, cols(j)].astype(f32)
            inner = s - mean_scaled - normed * mean_cross
            grad_buf[rows, cols(j)] = (out[rows, cols(j)].astype(f32) + inverse * inner).astype(jnp.bfloat16)
        store(i).start()
        return carry

    lax.fori_loop(0, steps, body, 0)
    for i in range(steps):
        store(i).wait()


def input_gradient(acts, up, out, gain, center_rows, inverse_rows):
    tokens = acts.shape[0]
    return pl.pallas_call(
        grad_kernel,
        in_specs=[pl.BlockSpec(memory_space=pltpu.HBM)] * 3 + [whole()] * 3,
        out_specs=pl.BlockSpec(memory_space=pltpu.HBM),
        out_shape=jax.ShapeDtypeStruct((tokens, D), jnp.bfloat16),
        scratch_shapes=[pltpu.VMEM((tokens, D), jnp.bfloat16)] * 4
        + [
            pltpu.SemaphoreType.DMA((3, tokens // TOKENS_STEP)),
            pltpu.SemaphoreType.DMA((tokens // TOKENS_STEP,)),
        ],
        compiler_params=params(),
        cost_estimate=pl.CostEstimate(flops=15 * tokens * D, bytes_accessed=8 * tokens * D, transcendentals=0),
    )(away(acts), away(up), away(out), gain.reshape(1, D), center_rows, inverse_rows)


def lane_index(rows):
    return lax.broadcasted_iota(jnp.int32, (rows, LANES), 1)


def position():
    layer = lax.axis_index("y") * 2 + lax.axis_index("xh")
    return layer, lax.axis_index("c"), lax.axis_index("xl"), lax.axis_index("zh"), lax.axis_index("zb")


def half_kernel(grid, half, sems):
    core = lax.axis_index("c")
    copies = [
        pltpu.make_async_copy(grid.at[i, 1 - core], half.at[i], sems.at[i]) for i in range(NODES // 2)
    ]
    for copy in copies:
        copy.start()
    for copy in copies:
        copy.wait()


def other_half(grid):
    return pl.pallas_call(
        half_kernel,
        in_specs=[pl.BlockSpec(memory_space=pltpu.HBM)],
        out_specs=whole(),
        out_shape=pltpu.VMEM((NODES // 2, NODE_ROWS, LANES), f32),
        scratch_shapes=[pltpu.SemaphoreType.DMA((NODES // 2,))],
        compiler_params=params(),
    )(away(grid))


def pair_kernel(own, other, parts, parts_other, result, total):
    core = lax.axis_index("c")
    count = NODES // 2
    last = count - 1
    high = lane_index(SHARD_ROWS) >= LANES // 2

    def add(i):
        total[0:NODE_ROWS, :] = (own[i] + other[i]) * SCALE
        total[NODE_ROWS : NODE_ROWS + 8, :] = jnp.zeros((8, LANES), f32)

    def pack(i):
        for xl in range(2):
            for z in range(8):
                base = QUARTER_ROWS * xl + PAIR_ROWS * (z // 2)
                if z % 2 == 0:
                    piece = total[base : base + SHARD_ROWS, :]
                else:
                    first = base + PAIR_ROWS // 2
                    ahead = total[first : first + SHARD_ROWS, :]
                    behind = total[first + 1 : first + 1 + SHARD_ROWS, :]
                    piece = pltpu.roll(jnp.where(high, ahead, behind), LANES // 2, 1)
                row = SHARD_ROWS * (z // 2)
                block = lax.rem(i, 2) * 16 + 8 * (z % 2) + 4 * xl + lax.div(i, 2)
                result[block, row : row + SHARD_ROWS, :] = piece

    def body(i, carry):
        add(i)
        pack(i)
        return carry

    lax.fori_loop(0, last, body, 0)
    add(last)

    def join(row, first, count):
        added = parts[first : first + count, :] + parts_other[first : first + count, :]
        sums = own[last, row : row + count, :] + other[last, row : row + count, :]
        total[row : row + count, :] = (sums + added) * PARTS_SCALE

    @pl.when(core == 0)
    def _():
        join(NODE_ROWS - COLS // 2, 0, COLS // 2)

    @pl.when(core == 1)
    def _():
        join(0, COLS // 2, 3 * COLS // 2)
        join(NODE_ROWS - COLS, 2 * COLS, COLS)

    pack(jnp.int32(last))


def pair_sum(own, other, parts, parts_other):
    return pl.pallas_call(
        pair_kernel,
        in_specs=[whole()] * 4,
        out_specs=whole(),
        out_shape=pltpu.VMEM((32, GROUP_ROWS, LANES), f32),
        scratch_shapes=[pltpu.VMEM((NODE_ROWS + 8, LANES), f32)],
        compiler_params=params(),
    )(held(own), held(other), held(parts), held(parts_other))


def place(rows):
    return lax.broadcasted_iota(jnp.int32, (rows, LANES), 0) * LANES + lane_index(rows)


def bounds_of(quarter):
    edges = BOUNDS + (LENGTH,)
    result = []
    for j in range(4):
        edge = jnp.int32(edges[j])
        for q in range(1, 4):
            edge = jnp.where(quarter == q, edges[2 * q + j] - q * QUARTER, edge)
        result.append(edge)
    return result


def moments(first, second, grad):
    new_first = beta_one * first + (1.0 - beta_one) * grad
    new_second = beta_two * second + (1.0 - beta_two) * grad * grad
    return new_first, new_second, new_first / (jnp.sqrt(new_second) + adam_epsilon)


def step_kernel(far, ours, ahead, behind, own_first, own_second, new_first, new_second, sent, table, own_update,
                grads, pieces):
    layer, core, xl, zh, zb = position()
    quarter = 2 * core + xl
    edges = bounds_of(quarter)
    for k, piece in enumerate((ours, ahead, far, behind)):
        pieces[k, :, :] = piece[...]
    source = [lax.rem(i + GROUP - zh, GROUP) for i in range(GROUP)]
    inside = place(SHARD_ROWS)
    valid = inside < SHARD
    weights = [jnp.zeros((SHARD_ROWS, LANES), f32) for _ in range(3)]
    updates = [jnp.zeros((SHARD_ROWS, LANES), f32) for _ in range(3)]
    for i in range(GROUP):
        rows = slice(SHARD_ROWS * i, SHARD_ROWS * (i + 1))
        offset = inside + (2 * i + zb) * SHARD
        place_in_layer = offset + quarter * QUARTER
        added = ((place_in_layer >= BOUNDS[4]) & (place_in_layer < BOUNDS[6])) | (place_in_layer >= BOUNDS[7])
        added = added & (layer == LAYERS - 1)
        total = pieces[source[0], rows, :]
        for k in range(1, GROUP):
            total = total + pieces[source[k], rows, :]
        grad = total * jnp.where(added, 1.0 / PARTS_SCALE, 1.0 / SCALE)
        grads[i, 0:SHARD_ROWS, :] = grad
        first, second, high, low = (
            pieces[source[i], GROUP_ROWS + SHARD_ROWS * k : GROUP_ROWS + SHARD_ROWS * (k + 1), :] for k in range(4)
        )
        update = moments(first, second, grad)[2]
        held = high + low * (1.0 / LOW_SCALE)
        sent[0, rows, :] = update
        sent[1, rows, :] = held
        for value, sums in ((held, weights), (update, updates)):
            square = jnp.where(valid, value * value, 0.0)
            for j in range(3):
                mask = (offset >= edges[j]) & (offset < edges[j + 1])
                sums[j] = sums[j] + jnp.where(mask, square, 0.0)
    lane = lane_index(1)
    row = jnp.zeros((1, LANES), f32)
    for base, sums in ((0, weights), (8, updates)):
        for j in range(3):
            column = jnp.sum(jnp.sum(sums[j], axis=0, keepdims=True), axis=1, keepdims=True)
            row = row + jnp.where(lane == base + 2 * quarter + j, column, 0.0)
    table[...] = jnp.broadcast_to(row, (64, LANES))
    first, second, update = moments(
        own_first[0:SHARD_ROWS, :], own_second[0:SHARD_ROWS, :], grads[zh, 0:SHARD_ROWS, :]
    )
    new_first[0:SHARD_ROWS, :] = first
    new_second[0:SHARD_ROWS, :] = second
    own_update[0:SHARD_ROWS, :] = update


def step(pieces, first, second):
    shard = jax.ShapeDtypeStruct((PIECE, LANES), f32)
    return pl.pallas_call(
        step_kernel,
        in_specs=[whole()] * 6,
        out_specs=[whole()] * 5,
        out_shape=[
            shard,
            shard,
            jax.ShapeDtypeStruct((2, GROUP_ROWS, LANES), f32),
            jax.ShapeDtypeStruct((64, LANES), f32),
            shard,
        ],
        scratch_shapes=[
            pltpu.VMEM((GROUP, PIECE, LANES), f32),
            pltpu.VMEM((GROUP, 2 * GROUP_ROWS, LANES), f32),
        ],
        compiler_params=params(),
    )(*pieces, first, second)


def layout_kernel(own, by_xl, by_zb, by_both, updates, masters, gathered, shifted):
    xl, zb = lax.axis_index("xl"), lax.axis_index("zb")
    groups = ((own, xl, zb), (by_xl, 1 - xl, zb), (by_zb, xl, 1 - zb), (by_both, 1 - xl, 1 - zb))
    low = lane_index(SHARD_ROWS) < LANES // 2
    for k, flat in enumerate((updates, masters)):
        for source, a, b in groups:
            for i in range(GROUP):
                rows = slice(SHARD_ROWS * i, SHARD_ROWS * (i + 1))
                gathered[8 * a + 2 * i + b, 0:SHARD_ROWS, :] = source[k, rows, :]
        for i in range(LOCALS // 2):
            base = PAIR_ROWS * i
            flat[base : base + 19, :] = gathered[2 * i, 0:19, :]
            shifted[0:1, :] = gathered[2 * i, 19:20, :]
            shifted[1:21, :] = pltpu.roll(gathered[2 * i + 1, 0:SHARD_ROWS, :], LANES // 2, 1)
            flat[base + 19 : base + 39, :] = jnp.where(low, shifted[0:20, :], shifted[1:21, :])


def layout(groups):
    return pl.pallas_call(
        layout_kernel,
        in_specs=[whole()] * 4,
        out_specs=[whole()] * 2,
        out_shape=[pltpu.VMEM((NODE_ROWS, LANES), f32)] * 2,
        scratch_shapes=[pltpu.VMEM((LOCALS, PIECE, LANES), f32), pltpu.VMEM((PIECE, LANES), f32)],
        compiler_params=params(),
    )(*groups)


def final_kernel(tables, updates, masters, master, update, new_master, new_params, trust, ratios):
    layer, core, xl, zh, zb = position()
    sums = tables[0:LAYERS, :]
    for n in range(1, 8):
        sums = sums + tables[LAYERS * n : LAYERS * (n + 1), :]
    roots = jnp.sqrt(sums)
    ratio = roots / (pltpu.roll(roots, LANES - 8, 1) + adam_epsilon)
    ratio = jnp.where(lane_index(8) < 8, ratio, 0.0)
    ratios[...] = ratio
    row = jnp.zeros((1, LANES), f32)
    for n in range(LAYERS):
        line = ratios[n : n + 1, :]
        row = row + (pltpu.roll(line, 8 * n, 1) if n else line)
    trust[...] = row[:, 0 : 8 * LAYERS]
    mine = ratios[pl.ds(layer, 1), :]
    lane = lane_index(1)
    values = [jnp.sum(jnp.where(lane == k, mine, 0.0), axis=1, keepdims=True) for k in range(8)]

    def spread(offset):
        factor = jnp.broadcast_to(values[0], offset.shape)
        for k in range(1, 8):
            factor = jnp.where(offset >= BOUNDS[k], values[k], factor)
        return factor

    start = core * NODE_PART
    index = 8 * xl + 2 * zh + zb
    new_master[0:SHARD_ROWS, :] = (
        master[0:SHARD_ROWS, :]
        - learn_rate * spread(place(SHARD_ROWS) + (start + index * SHARD)) * update[0:SHARD_ROWS, :]
    )
    step_rows = 104
    for i in range(NODE_ROWS // step_rows):
        rows = slice(step_rows * i, step_rows * (i + 1))
        factor = spread(place(step_rows) + (start + i * step_rows * LANES))
        new_params[rows, :] = (masters[rows, :] - learn_rate * factor * updates[rows, :]).astype(jnp.bfloat16)


def finish(tables, updates, masters, master, update):
    return pl.pallas_call(
        final_kernel,
        in_specs=[whole()] * 5,
        out_specs=[whole()] * 3,
        out_shape=[
            jax.ShapeDtypeStruct((PIECE, LANES), f32),
            jax.ShapeDtypeStruct((NODE_ROWS, LANES), jnp.bfloat16),
            jax.ShapeDtypeStruct((1, 8 * LAYERS), f32),
        ],
        scratch_shapes=[pltpu.VMEM((LAYERS, LANES), f32)],
        compiler_params=params(),
    )(tables, updates, masters, master, update)


def padded(vector):
    return jnp.pad(vector, (0, PIECE * LANES - SHARD)).reshape(PIECE, LANES)


def local(partials, master, first, second, acts, up_cot, out_cot, ln_gain):
    swap = ((0, 1), (1, 0))
    grid = partials.reshape(NODES // 2, 2, NODE_ROWS, LANES)
    sent = other_half(grid)
    other = lax.ppermute(sent, "c", swap)
    parts, center_rows, inverse_rows, own = token_sums(acts, up_cot, out_cot, grid)
    parts_other = lax.ppermute(parts, "c", swap)
    chunks = pair_sum(own, other, parts, parts_other)
    chunks = chunks.astype(f16)

    master, first, second = padded(master), padded(first), padded(second)
    high = master.astype(f16)
    low = ((master - high.astype(f32)) * LOW_SCALE).astype(f16)
    states = [v[0:SHARD_ROWS, :] for v in (first.astype(f16), second.astype(f16), high, low)]
    states = jnp.concatenate(states, axis=0)
    chunks, states, master, first, second = lax.optimization_barrier((chunks, states, master, first, second))
    blocks = lax.all_to_all(chunks, ("xh", "zb", "xl", "y"), 0, 0, tiled=True)
    plane = jnp.sum(blocks.astype(f32), axis=0).astype(f16)
    message = jnp.concatenate([plane, states], axis=0)
    far = lax.ppermute(message, "zh", [(i, i ^ 2) for i in range(GROUP)])
    near = [lax.ppermute(message, "zh", [(i, (i + k) % GROUP) for i in range(GROUP)]) for k in (1, 3)]
    pieces = [far, message, near[1], near[0]]
    pieces = [piece.astype(f32) for piece in pieces]
    new_first, new_second, stepped, table, update = step(pieces, first, second)
    table, center_rows, inverse_rows = lax.optimization_barrier((table, center_rows, inverse_rows))
    input_grad = input_gradient(acts, up_cot, out_cot, ln_gain, center_rows, inverse_rows)
    groups = [
        stepped,
        lax.ppermute(stepped, "xl", swap),
        lax.ppermute(stepped, "zb", swap),
        lax.ppermute(stepped, ("xl", "zb"), ((0, 3), (3, 0), (1, 2), (2, 1))),
    ]
    tables = lax.all_to_all(table.reshape(64, 1, LANES), ("c", "xl", "zb", "y", "xh"), 0, 0, tiled=True)
    updates, masters = layout(groups)
    new_master, new_params, trust = finish(tables.reshape(64, LANES), updates, masters, master, update)

    def flat(piece):
        return piece.reshape(PIECE * LANES)[:SHARD]

    return (
        flat(new_master),
        flat(new_first),
        flat(new_second),
        new_params.reshape(NODE_PART),
        trust.reshape(8 * LAYERS),
        input_grad,
    )


def solution(mesh):
    every = ("y", "xh", "c", "xl", "zh", "zb")
    fine = Mesh(mesh.devices.reshape(4, 2, 2, 2, 4, 2), every)
    in_specs = (P(every, None), P(every), P(every), P(every), P(every, None), P(every, None), P(every, None), P())
    out_specs = (P(every), P(every), P(every), P(("y", "xh", "c")), P(), P(every, None))
    return jax.shard_map(local, mesh=fine, in_specs=in_specs, out_specs=out_specs, check_vma=False)
```
